32 devices in a mesh: groups: 2 (over y), hosts: 8 (over z, x), tensor: 2 (over core).
Axes of the slice: x: 2, y: 2, z: 4, core: 2. Of those that a mesh axis runs over, the one named last changes fastest.
Arguments:
- context_queries: bfloat16 [2048, 8192], P(('groups', 'hosts'), 'tensor'), parts along dimension 0, may hold values from -6 to 6
- context_keys: bfloat16 [2048, 1024], P(('groups', 'hosts'), 'tensor'), parts along dimension 0, may hold values from -6 to 6
- context_values: bfloat16 [2048, 1024], P(('groups', 'hosts'), 'tensor'), parts along dimension 0, may hold values from -6 to 6
- doc_ids: int32 [2048], P(('groups', 'hosts')), parts along dimension 0, may hold values from 0 to 31, never falling along the last dimension, each value on 1 to 128 neighbouring positions
- query_token_rows: bfloat16 [16, 8192], P(('groups', 'hosts'), 'tensor'), parts along dimension 0, may hold values from -6 to 6
- span_start: int32 [16], P(('groups', 'hosts')), parts along dimension 0, may hold values from 0 to 511
Outputs:
- block_out: bfloat16 [2048, 8192], P(('groups', 'hosts'), 'tensor'), parts along dimension 0
- answer: bfloat16 [16, 8192], P(('groups', 'hosts'), 'tensor'), parts along dimension 0
The draws below stay inside these ranges and needn't reach their ends.
There are 2 independent parts, one for each index of `groups`. The reference program is written for one: setup_inputs(seed, part) draws one part's arguments, and reference() takes and returns one part's arrays. A program takes and returns all parts, laid end to end along the dimension named above; each array names one. Nothing has to cross between parts.
All inputs are finite; a program needn't handle non-finite values.
Results may differ from the reference program's by a relative error of at most 0.0043.
Values may be sent and summed in bfloat16 or wider, within the bound.
No kernel may reach another device: no remote copies, remote signals or barrier semaphores. Data moves between devices by JAX's collectives and lax.ppermute only.
A program may use at most 64 MiB of HBM per device.

```python
import math
import jax
import jax.numpy as jnp
import numpy as np
from jax import lax

QUERY_HEADS = 64
KEY_VALUE_HEADS = 8
HEAD_SIZE = 128
BLOCK_TOKENS = 128
CONTEXT_TOKENS = 1024
QUERY_COUNT = 8
N_HOSTS = 8


def coarse_rows(key, count_rows, heads):
    return jnp.clip(jax.random.normal(jax.random.fold_in(key, 5), (count_rows, heads, HEAD_SIZE), jnp.float32), -6.0, 6.0)


def draw_context_keys(key, part):
    base_offset = coarse_rows(jax.random.fold_in(key, 11), CONTEXT_TOKENS, KEY_VALUE_HEADS)
    return base_offset.reshape(CONTEXT_TOKENS, KEY_VALUE_HEADS * HEAD_SIZE).astype(jnp.bfloat16)


def draw_context_queries(key, part):
    base_offset = coarse_rows(jax.random.fold_in(key, 13), CONTEXT_TOKENS, QUERY_HEADS)
    return base_offset.reshape(CONTEXT_TOKENS, QUERY_HEADS * HEAD_SIZE).astype(jnp.bfloat16)


def draw_query_token_rows(key, part):
    base_offset = coarse_rows(jax.random.fold_in(key, 17), QUERY_COUNT, QUERY_HEADS)
    return base_offset.reshape(QUERY_COUNT, QUERY_HEADS * HEAD_SIZE).astype(jnp.bfloat16)


def touch_ends(drawn, stream_key, low, high):
    extent = drawn.shape
    spot = [jax.random.randint(jax.random.fold_in(stream_key, axis), (), 0, extent[axis]) for axis in range(len(extent))]
    drawn = drawn.at[tuple(spot)].set(low)
    longest = extent.index(max(extent))
    spot[longest] = (spot[longest] + 1) % extent[longest]
    return drawn.at[tuple(spot)].set(high)


def levels(key, dims, shards, low, high):
    gain = 1.0
    for axis_at, shards_of in shards:
        heights = jax.random.uniform(jax.random.fold_in(jax.random.fold_in(key, 6), axis_at), (shards_of,), jnp.float32, low / len(shards), high / len(shards))
        gain = gain * jnp.repeat(jnp.exp(heights), dims[axis_at] // shards_of).reshape((-1,) + (1,) * (len(dims) - 1 - axis_at))
    return gain


def split_up(count, total, most, lean):
    weights = [(1 << 20) // math.isqrt(grade ** lean) + 1 for grade in range(2, count + 1)]
    rest, holding = total - most - (count - 1), [1] * (count - 1)
    while rest > 0:
        movable = [i for i in range(count - 1) if holding[i] < most]
        pool, left = sum([weights[i] for i in movable]), rest
        for i in movable:
            extra = min(most - holding[i], max(1, left * weights[i] // pool), rest)
            holding[i] = holding[i] + extra
            rest = rest - extra
    return np.array([most] + holding)


def ragged_sizes(rng, number_of, total, bound, lean):
    if number_of == 2:
        one = jax.random.randint(rng, (), max(1, total - bound), min(bound, total - 1) + 1)
        return jnp.stack([one, total - one])
    sizes = jnp.asarray(split_up(number_of, total, bound, lean), jnp.int32)
    couples = (number_of - 1) // 2
    giver, taker = sizes[1:1 + 2 * couples:2], sizes[2:2 + 2 * couples:2]
    room = jnp.minimum(giver - 1, bound - taker)
    shifted = jax.random.randint(jax.random.fold_in(rng, 1), (couples,), 0, 1 << 20) % (room + 1)
    sizes = sizes.at[1:1 + 2 * couples:2].set(giver - shifted).at[2:2 + 2 * couples:2].set(taker + shifted)
    return sizes[jax.random.permutation(jax.random.fold_in(rng, 2), number_of)]


def scatter_about(key, dims, scale, reach, cuts=(), kind=jnp.bfloat16):
    loudness = levels(key, dims, cuts, -0.22, 0.18) if cuts else 1.0
    drawn = jax.random.normal(key, dims, jnp.float32) * scale * loudness
    return jnp.minimum(jnp.maximum(drawn, -reach), reach).astype(kind)


def setup_inputs(seed: int = 0, part: int = 0) -> dict:
    arg_keys = jax.random.split(jax.random.key(seed), 7)
    part_splits = jax.random.split(jax.random.fold_in(arg_keys[6], part), 7)
    return {
        "context_queries": draw_context_queries(jax.random.fold_in(jax.random.fold_in(arg_keys[6], part), 71), part),
        "context_keys": draw_context_keys(jax.random.fold_in(jax.random.fold_in(arg_keys[6], part), 71), part),
        "context_values": scatter_about(part_splits[2], (CONTEXT_TOKENS, KEY_VALUE_HEADS * HEAD_SIZE), 1.0, 6.0, ((0, 8), (1, 2))),
        "doc_ids": jnp.searchsorted(jnp.cumsum(ragged_sizes(part_splits[3], 4 * N_HOSTS, CONTEXT_TOKENS, BLOCK_TOKENS, 2)), jnp.arange(CONTEXT_TOKENS), side="right").astype(jnp.int32),
        "query_token_rows": draw_query_token_rows(jax.random.fold_in(jax.random.fold_in(arg_keys[6], part), 71), part),
        "span_start": touch_ends(jax.random.randint(part_splits[5], (QUERY_COUNT,), 0, CONTEXT_TOKENS // 2), jax.random.fold_in(part_splits[5], 1), 0, (CONTEXT_TOKENS // 2) - 1).astype(jnp.int32),
    }


MASKED_SCORE = -1e30


def reference(context_queries, context_keys, context_values, doc_ids, query_token_rows, span_start):
    factor = float(HEAD_SIZE) ** -0.5
    heads_per_group = QUERY_HEADS // KEY_VALUE_HEADS
    queries_of_block = context_queries.reshape(N_HOSTS, BLOCK_TOKENS, KEY_VALUE_HEADS, heads_per_group, HEAD_SIZE)
    keys_of_block = context_keys.reshape(N_HOSTS, BLOCK_TOKENS, KEY_VALUE_HEADS, HEAD_SIZE)
    values_of_block = context_values.reshape(N_HOSTS, BLOCK_TOKENS, KEY_VALUE_HEADS, HEAD_SIZE)
    block_docs = doc_ids.reshape(N_HOSTS, BLOCK_TOKENS)
    anchor_keys = keys_of_block[0]
    anchor_values = values_of_block[0]
    positions = jnp.arange(BLOCK_TOKENS, dtype=jnp.int32)
    causal = positions[None, :] <= positions[:, None]

    def block_pass(operands):
        block_index, query_part, key_part, value_part, doc_part = operands
        key_rows = jnp.concatenate([anchor_keys, key_part], 0).astype(jnp.float32)
        value_rows = jnp.concatenate([anchor_values, value_part], 0).astype(jnp.float32)
        own_visible = causal & (doc_part[:, None] == doc_part[None, :])
        front_visible = jnp.broadcast_to(block_index > 0, (BLOCK_TOKENS, BLOCK_TOKENS))
        visible = jnp.concatenate([front_visible, own_visible], 1)[:, None, None, :]
        scores = jnp.einsum('rkgd,skd->rkgs', query_part.astype(jnp.float32), key_rows) * factor
        peak_score = jnp.max(jnp.where(visible, scores, MASKED_SCORE), -1, keepdims=True)
        weights = jnp.where(visible, jnp.exp(scores - peak_score), 0.0)
        totals = jnp.sum(weights, -1)
        rounded = lax.optimization_barrier(weights.astype(jnp.bfloat16)).astype(jnp.float32)
        output = jnp.einsum('rkgs,skd->rkgd', rounded, value_rows) / totals[..., None]
        return output.astype(jnp.bfloat16).reshape(BLOCK_TOKENS, QUERY_HEADS * HEAD_SIZE)

    block_out = lax.map(block_pass, (jnp.arange(N_HOSTS, dtype=jnp.int32), queries_of_block, keys_of_block, values_of_block, block_docs))
    block_out = block_out.reshape(CONTEXT_TOKENS, QUERY_HEADS * HEAD_SIZE)

    query_single = query_token_rows.reshape(QUERY_COUNT, KEY_VALUE_HEADS, heads_per_group, HEAD_SIZE).astype(jnp.float32)

    def query_pass(running, operands):
        block_index, key_part, value_part = operands
        old_peak, old_total, old_acc = running
        scores = jnp.einsum('qkgd,skd->qkgs', query_single, key_part.astype(jnp.float32)) * factor
        key_positions = block_index * BLOCK_TOKENS + positions
        visible = (key_positions[None, :] >= span_start[:, None])[:, None, None, :]
        peak_score = jnp.max(jnp.where(visible, scores, MASKED_SCORE), -1)
        weights = jnp.where(visible, jnp.exp(scores - peak_score[..., None]), 0.0)
        totals = jnp.sum(weights, -1)
        rounded = lax.optimization_barrier(weights.astype(jnp.bfloat16)).astype(jnp.float32)
        partial_acc = jnp.einsum('qkgs,skd->qkgd', rounded, value_part.astype(jnp.float32))
        fresh = jnp.maximum(old_peak, peak_score)
        old_scale = jnp.exp(old_peak - fresh)
        new_scale = jnp.exp(peak_score - fresh)
        return (fresh, old_total * old_scale + totals * new_scale,
                old_acc * old_scale[..., None] + partial_acc * new_scale[..., None]), None

    start_offset = (jnp.full((QUERY_COUNT, KEY_VALUE_HEADS, heads_per_group), MASKED_SCORE, jnp.float32),
             jnp.zeros((QUERY_COUNT, KEY_VALUE_HEADS, heads_per_group), jnp.float32),
             jnp.zeros((QUERY_COUNT, KEY_VALUE_HEADS, heads_per_group, HEAD_SIZE), jnp.float32))
    final, unused = lax.scan(query_pass, start_offset, (jnp.arange(N_HOSTS, dtype=jnp.int32), keys_of_block, values_of_block))
    answer = (final[2] / final[1][..., None]).astype(jnp.bfloat16).reshape(QUERY_COUNT, QUERY_HEADS * HEAD_SIZE)
    return block_out, answer
```

```python
import functools

import jax
import jax.numpy as jnp
from jax import lax
from jax.experimental import pallas as pl
from jax.experimental.pallas import tpu as pltpu
from jax.sharding import PartitionSpec as P

HEAD_SIZE = 128
MASKED_SCORE = -1e30
FACTOR = float(HEAD_SIZE) ** -0.5
LOG2E = 1.4426950408889634
VMEM = pl.BlockSpec(memory_space=pltpu.VMEM)
SMEM = pl.BlockSpec(memory_space=pltpu.SMEM)
NT = (((1,), (1,)), ((), ()))


def dot_nt(a, b):
    return lax.dot_general(a, b, NT, preferred_element_type=jnp.float32)


def dot_nn(a, b):
    return jnp.dot(a, b, preferred_element_type=jnp.float32)


def prepare_kernel(span_ref, query_ref, key_ref, value_ref, message_ref, *piece_refs):
    heads = query_ref.shape[1] // HEAD_SIZE
    query = query_ref[...].astype(jnp.float32)
    for head in range(heads):
        message_ref[head : head + 1, :] = query[:, head * HEAD_SIZE : (head + 1) * HEAD_SIZE]
    start = span_ref[0].astype(jnp.float32)
    message_ref[heads : heads + 8, :] = jnp.full((8, HEAD_SIZE), start, jnp.float32)
    for index, piece_ref in enumerate(piece_refs):
        columns = slice(index * HEAD_SIZE, (index + 1) * HEAD_SIZE)
        rows = key_ref.shape[0]
        piece_ref[:rows, :] = key_ref[:, columns]
        piece_ref[rows:, :] = value_ref[:, columns]


def prepare(query_row, span, keys, values):
    heads = query_row.shape[1] // HEAD_SIZE
    kv_count = keys.shape[1] // HEAD_SIZE
    rows = keys.shape[0]
    piece = jax.ShapeDtypeStruct((2 * rows, HEAD_SIZE), keys.dtype)
    return pl.pallas_call(
        prepare_kernel,
        out_shape=[jax.ShapeDtypeStruct((heads + 8, HEAD_SIZE), jnp.float32)] + [piece] * kv_count,
        in_specs=[SMEM, VMEM, VMEM, VMEM],
        out_specs=[VMEM] * (1 + kv_count),
        cost_estimate=pl.CostEstimate(flops=1000, bytes_accessed=600000, transcendentals=0),
        name="prepare",
    )(span, query_row, keys, values)


def partials_kernel(host_ref, k0_ref, v0_ref, k1_ref, v1_ref, *refs):
    sources = len(refs) // 2
    message_refs, out_refs = refs[:sources], refs[sources:]
    block = k0_ref.shape[0]
    kv_count = k0_ref.shape[1] // HEAD_SIZE
    heads = message_refs[0].shape[0] - 8
    per_kv = heads // kv_count
    rows = sources * heads
    host = host_ref[0]
    queries = jnp.concatenate([ref[:heads, :] for ref in message_refs], 0).astype(jnp.bfloat16)
    starts = jnp.concatenate(
        [jnp.broadcast_to(ref[heads : heads + 1, :], (heads, HEAD_SIZE)) for ref in message_refs], 0
    )
    row_kv = (lax.broadcasted_iota(jnp.int32, (rows, HEAD_SIZE), 0) % heads) // per_kv
    lanes = lax.broadcasted_iota(jnp.int32, (rows, block), 1)

    def chosen(per_head):
        out = per_head[0]
        for index in range(1, kv_count):
            out = jnp.where(row_kv == index, per_head[index], out)
        return out

    scores, shown = [], []
    for key_ref, at in ((k0_ref, host), (k1_ref, host ^ 1)):
        scores.append(
            chosen(
                [
                    dot_nt(queries, key_ref[:, h * HEAD_SIZE : (h + 1) * HEAD_SIZE])
                    for h in range(kv_count)
                ]
            )
            * FACTOR
        )
        shown.append((lanes + at * block).astype(jnp.float32) >= starts)
    masked = [jnp.where(s, x, MASKED_SCORE) for s, x in zip(shown, scores)]
    peak = jnp.max(jnp.maximum(masked[0], masked[1]), -1, keepdims=True)
    weights = [
        jnp.where(s, jnp.exp2((x - peak) * LOG2E), 0.0) for s, x in zip(shown, masked)
    ]
    total = jnp.sum(weights[0] + weights[1], -1, keepdims=True)
    rounded = [w.astype(jnp.bfloat16) for w in weights]
    acc = chosen(
        [
            dot_nn(rounded[0], v0_ref[:, h * HEAD_SIZE : (h + 1) * HEAD_SIZE])
            + dot_nn(rounded[1], v1_ref[:, h * HEAD_SIZE : (h + 1) * HEAD_SIZE])
            for h in range(kv_count)
        ]
    )
    peak_row = jnp.transpose(jnp.broadcast_to(peak, (rows, HEAD_SIZE)))[0:1, :]
    total_row = jnp.transpose(jnp.broadcast_to(total, (rows, HEAD_SIZE)))[0:1, :]
    for index, out_ref in enumerate(out_refs):
        out_ref[:heads, :] = acc[index * heads : (index + 1) * heads, :]
        out_ref[heads : heads + 1, :] = peak_row[:, :HEAD_SIZE]
        out_ref[heads + 1 : heads + 2, :] = total_row[:, :HEAD_SIZE]
        out_ref[heads + 2 : heads + 8, :] = jnp.zeros((6, HEAD_SIZE), jnp.float32)


def partials(host, k0, v0, k1, v1, messages):
    shape = jax.ShapeDtypeStruct(messages[0].shape, jnp.float32)
    return pl.pallas_call(
        partials_kernel,
        out_shape=[shape] * len(messages),
        in_specs=[SMEM] + [VMEM] * (4 + len(messages)),
        out_specs=[VMEM] * len(messages),
        cost_estimate=pl.CostEstimate(flops=1000000, bytes_accessed=900000, transcendentals=40000),
        name="query_partials",
    )(host, k0, v0, k1, v1, *messages)


def merge_kernel(*refs):
    part_refs, answer_ref = refs[:-1], refs[-1]
    heads = part_refs[0].shape[0] - 8
    row = lax.broadcasted_iota(jnp.int32, (heads, HEAD_SIZE), 0)
    lane = lax.broadcasted_iota(jnp.int32, (heads, HEAD_SIZE), 1)

    def column(ref, at, index):
        spread = jnp.broadcast_to(ref[at : at + 1, :], (heads, HEAD_SIZE))
        return jnp.sum(jnp.where(lane == row + index * heads, spread, 0.0), -1, keepdims=True)

    peaks = [column(ref, heads, index) for index, ref in enumerate(part_refs)]
    totals = [column(ref, heads + 1, index) for index, ref in enumerate(part_refs)]
    peak = functools.reduce(jnp.maximum, peaks)
    scales = [jnp.exp(p - peak) for p in peaks]
    total = functools.reduce(jnp.add, [s * t for s, t in zip(scales, totals)])
    merged = functools.reduce(
        jnp.add, [s * ref[:heads, :] for s, ref in zip(scales, part_refs)]
    )
    answer = (merged / total).astype(answer_ref.dtype)
    for head in range(heads):
        answer_ref[:, head * HEAD_SIZE : (head + 1) * HEAD_SIZE] = answer[head : head + 1, :]


def merge(parts):
    heads = parts[0].shape[0] - 8
    return pl.pallas_call(
        merge_kernel,
        out_shape=jax.ShapeDtypeStruct((1, heads * HEAD_SIZE), jnp.bfloat16),
        in_specs=[VMEM] * len(parts),
        out_specs=VMEM,
        cost_estimate=pl.CostEstimate(flops=100000, bytes_accessed=90000, transcendentals=1000),
        name="merge_answer",
    )(*parts)


def context_kernel(
    host_ref, column_ref, doc_ref, query_ref, key_ref, value_ref, *refs
):
    piece_refs, out_ref, bias_ref = refs[:-2], refs[-2], refs[-1]
    step = pl.program_id(0)
    block = query_ref.shape[0]
    heads = query_ref.shape[1] // HEAD_SIZE
    scale = FACTOR * LOG2E

    @pl.when(step == 0)
    def _():
        row = lax.broadcasted_iota(jnp.int32, (block, block), 0)
        lane = lax.broadcasted_iota(jnp.int32, (block, block), 1)
        along = jnp.broadcast_to(doc_ref[...].astype(jnp.float32), (block, block))
        visible = (lane <= row) & (jnp.transpose(along) == along)
        bias_ref[...] = jnp.where(visible, 0.0, MASKED_SCORE)

    anchor = piece_refs[0][...]
    for index in range(1, len(piece_refs)):
        anchor = jnp.where(step == index, piece_refs[index][...], anchor)
    anchor_keys, anchor_values = anchor[:block, :], anchor[block:, :]
    bias = bias_ref[...]
    front = jnp.where(host_ref[0] > 0, 0.0, MASKED_SCORE)
    keys = key_ref[...]
    values = jnp.concatenate([value_ref[...], anchor_values], 0)
    values = jnp.concatenate([values, jnp.ones((2 * block, HEAD_SIZE), values.dtype)], 1)
    for head in range(heads):
        columns = slice(head * HEAD_SIZE, (head + 1) * HEAD_SIZE)
        query = query_ref[:, columns]
        own = dot_nt(query, keys) + bias
        far = dot_nt(query, anchor_keys) + front
        peak = jnp.max(jnp.maximum(own, far), -1, keepdims=True)
        weights = jnp.concatenate(
            [
                jnp.exp2((own - peak) * scale).astype(jnp.bfloat16),
                jnp.exp2((far - peak) * scale).astype(jnp.bfloat16),
            ],
            1,
        )
        sums = dot_nn(weights, values)
        out_ref[:, columns] = (sums[:, :HEAD_SIZE] / sums[:, HEAD_SIZE:]).astype(out_ref.dtype)


def context_attention(host, column, doc_row, queries, keys, values, pieces):
    block, width = queries.shape
    kv_count = keys.shape[1] // HEAD_SIZE
    group = width // kv_count

    def head_of(step, host_ref, column_ref):
        return (0, step ^ column_ref[0])

    whole = pl.BlockSpec(pieces[0].shape, lambda step, *_: (0, 0))
    return pl.pallas_call(
        context_kernel,
        out_shape=jax.ShapeDtypeStruct((block, width), queries.dtype),
        grid_spec=pltpu.PrefetchScalarGridSpec(
            num_scalar_prefetch=2,
            grid=(kv_count,),
            in_specs=[
                pl.BlockSpec((1, block), lambda step, *_: (0, 0)),
                pl.BlockSpec((block, group), head_of),
                pl.BlockSpec((block, HEAD_SIZE), head_of),
                pl.BlockSpec((block, HEAD_SIZE), head_of),
            ]
            + [whole] * len(pieces),
            out_specs=pl.BlockSpec((block, group), head_of),
            scratch_shapes=[pltpu.VMEM((block, block), jnp.float32)],
        ),
        cost_estimate=pl.CostEstimate(
            flops=4 * block * 2 * block * width, bytes_accessed=2600000, transcendentals=1000000
        ),
        name="context_attention",
    )(host, column, doc_row, queries, keys, values, *pieces)


def paired(context_queries, context_keys, context_values, doc_ids, query_token_rows, span_start):
    host_count = lax.axis_size("hosts")
    host = lax.axis_index("hosts")
    depth = host_count // 2
    place, side = host // 2, host % 2
    block = context_queries.shape[0]

    def swap(value, mask):
        return lax.ppermute(value, "hosts", [(i, i ^ mask) for i in range(host_count)])

    message, *own_pieces = prepare(query_token_rows, span_start, context_keys, context_values)
    other_keys, other_values = swap(context_keys, 1), swap(context_values, 1)
    messages = [message] + [swap(message, 2 * k) for k in range(1, depth)]
    sent = [lax.ppermute(own_pieces[k], "hosts", [(0, 2 * k)]) for k in range(1, depth)]
    piece = jnp.where(place == 0, own_pieces[0], functools.reduce(jnp.add, sent))
    piece = jnp.where(side == 0, piece, swap(piece, 1))
    pieces = [piece] + [swap(piece, 2 * k) for k in range(1, depth)]
    host_word = host.reshape(1).astype(jnp.int32)
    parts = partials(
        host_word, context_keys, context_values, other_keys, other_values, messages
    )
    parts = [parts[0]] + [swap(parts[k], 2 * k) for k in range(1, depth)]
    answer = merge(parts)
    block_out = context_attention(
        host_word,
        place.reshape(1).astype(jnp.int32),
        doc_ids.reshape(1, block),
        context_queries,
        context_keys,
        context_values,
        pieces,
    )
    return block_out, answer


def from_root(value, axis, source):
    kept = jnp.where(lax.axis_index(axis) == source, value, 0).astype(value.dtype)
    return lax.psum(kept, axis)


def head_groups(matrix, kv_count):
    count_rows = matrix.shape[0]
    return matrix.reshape(
        count_rows, kv_count, matrix.shape[1] // (kv_count * HEAD_SIZE), HEAD_SIZE
    ).transpose(1, 0, 2, 3)


def kv_groups(matrix, kv_count):
    return matrix.reshape(matrix.shape[0], kv_count, HEAD_SIZE).transpose(1, 0, 2)


def query_partials(queries, key_rows, value_rows, visible):
    kv_count = key_rows.shape[1] // HEAD_SIZE

    def query_per_head(operands):
        query_part, key_part, value_part = operands
        scores = (
            jnp.einsum("qgd,sd->qgs", query_part, key_part, preferred_element_type=jnp.float32)
            * FACTOR
        )
        shown = visible[:, None, :]
        peak_score = jnp.max(jnp.where(shown, scores, MASKED_SCORE), -1)
        weights = jnp.where(shown, jnp.exp(scores - peak_score[..., None]), 0.0)
        totals = jnp.sum(weights, -1)
        partial_acc = jnp.einsum(
            "qgs,sd->qgd",
            weights.astype(jnp.bfloat16),
            value_part,
            preferred_element_type=jnp.float32,
        )
        return (peak_score, totals, partial_acc)

    peaks, totals, accums = lax.map(
        query_per_head,
        (
            head_groups(queries, kv_count),
            kv_groups(key_rows, kv_count),
            kv_groups(value_rows, kv_count),
        ),
    )
    query_count = queries.shape[0]
    peaks = peaks.transpose(1, 0, 2).reshape(query_count, -1)
    totals = totals.transpose(1, 0, 2).reshape(query_count, -1)
    accums = accums.transpose(1, 0, 2, 3).reshape(query_count, -1)
    return (peaks, totals, accums)


def gathered(context_queries, context_keys, context_values, doc_ids, query_token_rows, span_start):
    host = lax.axis_index("hosts")
    host_count = lax.axis_size("hosts")
    block = context_queries.shape[0]
    per_host = query_token_rows.shape[0]
    kv_count = context_keys.shape[1] // HEAD_SIZE
    anchor = from_root(jnp.stack([context_keys, context_values]), "hosts", 0)
    pieces = [
        anchor[:, :, h * HEAD_SIZE : (h + 1) * HEAD_SIZE].reshape(2 * block, HEAD_SIZE)
        for h in range(kv_count)
    ]
    block_out = context_attention(
        host.reshape(1).astype(jnp.int32),
        jnp.zeros((1,), jnp.int32),
        doc_ids.reshape(1, block),
        context_queries,
        context_keys,
        context_values,
        pieces,
    )
    all_queries, all_spans = (
        lax.all_gather(query_token_rows, "hosts", axis=0, tiled=True),
        lax.all_gather(span_start, "hosts", axis=0, tiled=True),
    )
    key_positions = host * block + jnp.arange(block, dtype=jnp.int32)
    query_visible = key_positions[None, :] >= all_spans[:, None]
    peaks, totals, accums = query_partials(
        all_queries, context_keys, context_values, query_visible
    )
    received = [
        lax.all_to_all(x, "hosts", split_axis=0, concat_axis=0, tiled=True).reshape(
            host_count, per_host, -1
        )
        for x in (peaks, totals, accums)
    ]
    source_peaks, source_totals, source_accums = received
    overall = jnp.max(source_peaks, 0)
    scales = jnp.exp(source_peaks - overall[None])
    own_totals = jnp.sum(scales * source_totals, 0)
    own_accums = jnp.sum(jnp.repeat(scales, HEAD_SIZE, axis=2) * source_accums, 0)
    answer = (own_accums / jnp.repeat(own_totals, HEAD_SIZE, axis=1)).astype(jnp.bfloat16)
    return (block_out, answer)


def solution(mesh):
    rows = P(("groups", "hosts"), "tensor")
    words = P(("groups", "hosts"))

    def on_device(context_queries, context_keys, context_values, doc_ids, query_rows, span_start):
        kv_count = context_keys.shape[1] // HEAD_SIZE
        fits = mesh.shape["hosts"] == 2 * kv_count and kv_count == 4 and query_rows.shape[0] == 1
        plan = paired if fits else gathered
        return plan(
            context_queries, context_keys, context_values, doc_ids, query_rows, span_start
        )

    return jax.shard_map(
        on_device,
        mesh=mesh,
        in_specs=(rows, rows, rows, words, rows, words),
        out_specs=(rows, rows),
        check_vma=False,
    )
```

```python
import functools

import jax
import jax.numpy as jnp
from jax import lax
from jax.experimental import pallas as pl
from jax.experimental.pallas import tpu as pltpu
from jax.sharding import PartitionSpec as P

HEAD_SIZE = 128
MASKED_SCORE = -1e30
FACTOR = float(HEAD_SIZE) ** -0.5
LOG2E = 1.4426950408889634
VMEM = pl.BlockSpec(memory_space=pltpu.VMEM)
SMEM = pl.BlockSpec(memory_space=pltpu.SMEM)
HBM = pl.BlockSpec(memory_space=pltpu.HBM)
SPAN_ROWS = 16
UNIT = 4
NT = (((1,), (1,)), ((), ()))


def in_hbm(x):
    return pltpu.with_memory_space_constraint(x, pltpu.HBM)


def dot_nt(a, b):
    return lax.dot_general(a, b, NT, preferred_element_type=jnp.float32)


def dot_nn(a, b):
    return jnp.dot(a, b, preferred_element_type=jnp.float32)


def span_rows(start):
    row = lax.broadcasted_iota(jnp.int32, (SPAN_ROWS, HEAD_SIZE), 0)
    start = jnp.broadcast_to(start, (SPAN_ROWS, HEAD_SIZE))
    digit = jnp.where(row < SPAN_ROWS // 2, start // HEAD_SIZE, start % HEAD_SIZE)
    return digit.astype(jnp.float32).astype(jnp.bfloat16)


def span_of(rows):
    digits = rows.astype(jnp.float32)
    return digits[0:1, :] * HEAD_SIZE + digits[SPAN_ROWS // 2 : SPAN_ROWS // 2 + 1, :]


def prepare_kernel(span_ref, query_ref, key_ref, value_ref, *refs):
    packet_refs, (row, keys, values, rows_ref, sems) = refs[:-5], refs[-5:]
    block, heads = key_ref.shape[0], query_ref.shape[1] // HEAD_SIZE
    copies = [
        pltpu.make_async_copy(source, target, sems.at[i])
        for i, (source, target) in enumerate(
            ((query_ref, row), (key_ref, keys), (value_ref, values))
        )
    ]
    for copy in copies:
        copy.start()
    copies.pop(0).wait()
    query = row[...].astype(jnp.float32)
    for head in range(heads):
        rows_ref[head : head + 1, :] = query[:, head * HEAD_SIZE : (head + 1) * HEAD_SIZE]
    query_rows = rows_ref[...].astype(jnp.bfloat16)
    span = span_rows(span_ref[...])
    for copy in copies:
        copy.wait()
    for index, packet_ref in enumerate(packet_refs):
        columns = slice(index * HEAD_SIZE, (index + 1) * HEAD_SIZE)
        packet_ref[:block, :] = keys[:, columns]
        packet_ref[block : 2 * block, :] = values[:, columns]
        packet_ref[2 * block : 2 * block + heads, :] = query_rows
        packet_ref[2 * block + heads :, :] = span


def prepare(query_row, span, keys, values):
    heads = query_row.shape[1] // HEAD_SIZE
    block, width = keys.shape
    packet = pltpu.VMEM((2 * block + heads + SPAN_ROWS, HEAD_SIZE), keys.dtype)
    pinned = [in_hbm(x) for x in (query_row, keys, values)]
    return pl.pallas_call(
        prepare_kernel,
        out_shape=[packet] * (width // HEAD_SIZE),
        in_specs=[VMEM, HBM, HBM, HBM],
        out_specs=[VMEM] * (width // HEAD_SIZE),
        scratch_shapes=[
            pltpu.VMEM(query_row.shape, query_row.dtype),
            pltpu.VMEM((block, width), keys.dtype),
            pltpu.VMEM((block, width), keys.dtype),
            pltpu.VMEM((heads, HEAD_SIZE), jnp.float32),
            pltpu.SemaphoreType.DMA((3,)),
        ],
        compiler_params=pltpu.CompilerParams(vmem_limit_bytes=8 * 2**20),
        cost_estimate=pl.CostEstimate(flops=1000, bytes_accessed=600000, transcendentals=0),
        name="prepare",
    )(span.reshape(1, 1), *pinned)


def own_bias(doc_row):
    block = doc_row.shape[1]
    row = lax.broadcasted_iota(jnp.int32, (block, block), 0)
    lane = lax.broadcasted_iota(jnp.int32, (block, block), 1)
    along = jnp.broadcast_to(doc_row.astype(jnp.float32), (block, block))
    return jnp.where((lane <= row) & (jnp.transpose(along) == along), 0.0, MASKED_SCORE)


def partials_kernel(
    host_ref, doc_ref, context_ref, k0_ref, v0_ref, k1_ref, v1_ref, *refs
):
    sources = (len(refs) - 3) // 2
    packet_refs, out_refs = refs[:sources], refs[sources : 2 * sources]
    staged_ref, bias_ref, sem = refs[-3:]
    staging = pltpu.make_async_copy(context_ref, staged_ref, sem)
    staging.start()
    bias_ref[...] = own_bias(doc_ref[...])
    block = k0_ref.shape[0]
    kv_count = k0_ref.shape[1] // HEAD_SIZE
    heads = packet_refs[0].shape[0] - 2 * block - SPAN_ROWS
    per_kv = heads // kv_count
    rows = sources * heads
    host = host_ref[0]
    queries = jnp.concatenate([ref[2 * block : 2 * block + heads, :] for ref in packet_refs], 0)
    starts = jnp.concatenate(
        [
            jnp.broadcast_to(span_of(ref[2 * block + heads :, :]), (heads, HEAD_SIZE))
            for ref in packet_refs
        ],
        0,
    )
    row_kv = (lax.broadcasted_iota(jnp.int32, (rows, HEAD_SIZE), 0) % heads) // per_kv
    lanes = lax.broadcasted_iota(jnp.int32, (rows, block), 1)

    def chosen(per_head):
        out = per_head[0]
        for index in range(1, kv_count):
            out = jnp.where(row_kv == index, per_head[index], out)
        return out

    scores, shown = [], []
    for key_ref, at in ((k0_ref, host), (k1_ref, host ^ 1)):
        scores.append(
            chosen(
                [
                    dot_nt(queries, key_ref[:, h * HEAD_SIZE : (h + 1) * HEAD_SIZE])
                    for h in range(kv_count)
                ]
            )
            * FACTOR
        )
        shown.append((lanes + at * block).astype(jnp.float32) >= starts)
    masked = [jnp.where(s, x, MASKED_SCORE) for s, x in zip(shown, scores)]
    peak = jnp.max(jnp.maximum(masked[0], masked[1]), -1, keepdims=True)
    weights = [
        jnp.where(s, jnp.exp2((x - peak) * LOG2E), 0.0) for s, x in zip(shown, masked)
    ]
    total = jnp.sum(weights[0] + weights[1], -1, keepdims=True)
    rounded = [w.astype(jnp.bfloat16) for w in weights]
    acc = chosen(
        [
            dot_nn(rounded[0], v0_ref[:, h * HEAD_SIZE : (h + 1) * HEAD_SIZE])
            + dot_nn(rounded[1], v1_ref[:, h * HEAD_SIZE : (h + 1) * HEAD_SIZE])
            for h in range(kv_count)
        ]
    )
    peak_row = jnp.transpose(jnp.broadcast_to(peak, (rows, HEAD_SIZE)))[0:1, :]
    total_row = jnp.transpose(jnp.broadcast_to(total, (rows, HEAD_SIZE)))[0:1, :]
    for index, out_ref in enumerate(out_refs):
        out_ref[:heads, :] = acc[index * heads : (index + 1) * heads, :]
        out_ref[heads : heads + 1, :] = peak_row[:, :HEAD_SIZE]
        out_ref[heads + 1 : heads + 2, :] = total_row[:, :HEAD_SIZE]
        out_ref[heads + 2 : heads + 8, :] = jnp.zeros((6, HEAD_SIZE), jnp.float32)
    staging.wait()


def partials(host, docs, context_queries, k0, v0, k1, v1, packets):
    block = k0.shape[0]
    heads = packets[0].shape[0] - 2 * block - SPAN_ROWS
    part = pltpu.VMEM((heads + 8, HEAD_SIZE), jnp.float32)
    staged = pltpu.VMEM(context_queries.shape, context_queries.dtype)
    bias = pltpu.VMEM((block, block), jnp.float32)
    return pl.pallas_call(
        partials_kernel,
        out_shape=[part] * len(packets) + [staged, bias],
        in_specs=[SMEM, VMEM, HBM] + [VMEM] * (4 + len(packets)),
        out_specs=[VMEM] * (len(packets) + 2),
        scratch_shapes=[pltpu.SemaphoreType.DMA],
        compiler_params=pltpu.CompilerParams(vmem_limit_bytes=8 * 2**20),
        cost_estimate=pl.CostEstimate(flops=1000000, bytes_accessed=900000, transcendentals=40000),
        name="query_partials",
    )(host, docs.reshape(1, block), in_hbm(context_queries), k0, v0, k1, v1, *packets)


def merge_kernel(*refs):
    part_refs, answer_ref = refs[:-1], refs[-1]
    heads = part_refs[0].shape[0] - 8
    row = lax.broadcasted_iota(jnp.int32, (heads, HEAD_SIZE), 0)
    lane = lax.broadcasted_iota(jnp.int32, (heads, HEAD_SIZE), 1)

    def column(ref, at, index):
        spread = jnp.broadcast_to(ref[at : at + 1, :], (heads, HEAD_SIZE))
        return jnp.sum(jnp.where(lane == row + index * heads, spread, 0.0), -1, keepdims=True)

    peaks = [column(ref, heads, index) for index, ref in enumerate(part_refs)]
    totals = [column(ref, heads + 1, index) for index, ref in enumerate(part_refs)]
    peak = functools.reduce(jnp.maximum, peaks)
    scales = [jnp.exp(p - peak) for p in peaks]
    total = functools.reduce(jnp.add, [s * t for s, t in zip(scales, totals)])
    merged = functools.reduce(
        jnp.add, [s * ref[:heads, :] for s, ref in zip(scales, part_refs)]
    )
    answer = (merged / total).astype(answer_ref.dtype)
    for head in range(heads):
        answer_ref[:, head * HEAD_SIZE : (head + 1) * HEAD_SIZE] = answer[head : head + 1, :]


def merge(parts):
    heads = parts[0].shape[0] - 8
    return pl.pallas_call(
        merge_kernel,
        out_shape=jax.ShapeDtypeStruct((1, heads * HEAD_SIZE), jnp.bfloat16),
        in_specs=[VMEM] * len(parts),
        out_specs=VMEM,
        compiler_params=pltpu.CompilerParams(vmem_limit_bytes=8 * 2**20),
        cost_estimate=pl.CostEstimate(flops=100000, bytes_accessed=90000, transcendentals=1000),
        name="merge_answer",
    )(*parts)


def context_kernel(host_ref, column_ref, bias_ref, query_ref, key_ref, value_ref, *refs):
    piece_refs, out_ref, held, sems = refs[:-3], refs[-3], refs[-2], refs[-1]
    block = query_ref.shape[0]
    group = held.shape[2] // HEAD_SIZE
    scale = FACTOR * LOG2E
    front = jnp.where(host_ref[0] > 0, 0.0, MASKED_SCORE)
    bias = jnp.concatenate([bias_ref[...], jnp.full((block, block), front, jnp.float32)], 1)
    bias = jnp.concatenate([bias] * UNIT, 0)
    ones = jnp.ones((2 * block, HEAD_SIZE), jnp.bfloat16)

    def lanes(index, width):
        return pl.ds(pl.multiple_of((index ^ column_ref[0]) * width, HEAD_SIZE), width)

    def score(index, head):
        at = lanes(index, group * HEAD_SIZE)
        query = jnp.concatenate(
            [
                query_ref[:, pl.ds(at.start + (head + i) * HEAD_SIZE, HEAD_SIZE)]
                for i in range(UNIT)
            ],
            0,
        )
        keys = jnp.concatenate(
            [key_ref[:, lanes(index, HEAD_SIZE)], piece_refs[index][:block, :]], 0
        )
        return dot_nt(query, keys)

    def weigh(scores):
        scores = scores + bias
        peak = jnp.max(scores, -1, keepdims=True)
        return jnp.exp2((scores - peak) * scale).astype(jnp.bfloat16)

    def gather(index, weights):
        values = jnp.concatenate(
            [value_ref[:, lanes(index, HEAD_SIZE)], piece_refs[index][block : 2 * block, :]], 0
        )
        return dot_nn(weights, jnp.concatenate([values, ones], 1))

    def finish(index, head, sums):
        total = sums[:, HEAD_SIZE:]
        inverse = pl.reciprocal(total, approx=True)
        inverse = inverse * (2.0 - total * inverse)
        out = (sums[:, :HEAD_SIZE] * inverse).astype(jnp.bfloat16)
        for i in range(UNIT):
            columns = slice((head + i) * HEAD_SIZE, (head + i + 1) * HEAD_SIZE)
            held[index, :, columns] = out[i * block : (i + 1) * block, :]

    units = [(k, g) for k in range(len(piece_refs)) for g in range(0, group, UNIT)]
    scores, weights, sums, copies = {}, {}, {}, []
    for step in range(len(units) + 3):
        if step >= 3:
            index, head = units[step - 3]
            finish(index, head, sums.pop(step - 3))
            if head + UNIT == group:
                copies.append(
                    pltpu.make_async_copy(
                        held.at[index],
                        out_ref.at[:, lanes(index, group * HEAD_SIZE)],
                        sems.at[index],
                    )
                )
                copies[-1].start()
        if 2 <= step < len(units) + 2:
            sums[step - 2] = gather(units[step - 2][0], weights.pop(step - 2))
        if 1 <= step < len(units) + 1:
            weights[step - 1] = weigh(scores.pop(step - 1))
        if step < len(units):
            scores[step] = score(*units[step])
    for copy in copies:
        copy.wait()


def context_attention(host, column, bias, queries, keys, values, pieces):
    block, width = queries.shape
    kv_count = len(pieces)
    return pl.pallas_call(
        context_kernel,
        out_shape=jax.ShapeDtypeStruct((block, width), queries.dtype),
        in_specs=[SMEM, SMEM] + [VMEM] * (4 + kv_count),
        out_specs=HBM,
        scratch_shapes=[
            pltpu.VMEM((kv_count, block, width // kv_count), queries.dtype),
            pltpu.SemaphoreType.DMA((kv_count,)),
        ],
        compiler_params=pltpu.CompilerParams(vmem_limit_bytes=24 * 2**20),
        cost_estimate=pl.CostEstimate(
            flops=4 * block * 2 * block * width, bytes_accessed=2600000, transcendentals=1000000
        ),
        name="context_attention",
    )(host, column, bias, queries, keys, values, *pieces)


def paired(context_queries, context_keys, context_values, doc_ids, query_token_rows, span_start):
    host_count = lax.axis_size("hosts")
    host = lax.axis_index("hosts")
    depth = host_count // 2
    place, side = host // 2, host % 2
    block = context_queries.shape[0]

    def swap(value, mask):
        return lax.ppermute(value, "hosts", [(i, i ^ mask) for i in range(host_count)])

    packets = prepare(query_token_rows, span_start, context_keys, context_values)
    other_keys, other_values = swap(context_keys, 1), swap(context_values, 1)
    packets = [packets[0]] + [swap(packets[k], 2 * k) for k in range(1, depth)]
    other_keys, other_values, *packets = lax.optimization_barrier(
        (other_keys, other_values, *packets)
    )
    piece = packets[0][: 2 * block]
    for k in range(1, depth):
        piece = jnp.where(place == k, packets[k][: 2 * block], piece)
    crossed = swap(piece, 1)
    host_word = host.reshape(1).astype(jnp.int32)
    *parts, staged, bias = partials(
        host_word,
        doc_ids,
        context_queries,
        context_keys,
        context_values,
        other_keys,
        other_values,
        packets,
    )
    crossed, *parts = lax.optimization_barrier((crossed, *parts))
    parts = [parts[0]] + [swap(parts[k], 2 * k) for k in range(1, depth)]
    piece = jnp.where(side == 0, piece, crossed)
    pieces = [piece] + [swap(piece, 2 * k) for k in range(1, depth)]
    answer = merge(parts)
    block_out = context_attention(
        host_word,
        place.reshape(1).astype(jnp.int32),
        bias,
        staged,
        context_keys,
        context_values,
        pieces,
    )
    return block_out, answer


def from_root(value, axis, source):
    kept = jnp.where(lax.axis_index(axis) == source, value, 0).astype(value.dtype)
    return lax.psum(kept, axis)


def head_groups(matrix, kv_count):
    count_rows = matrix.shape[0]
    return matrix.reshape(
        count_rows, kv_count, matrix.shape[1] // (kv_count * HEAD_SIZE), HEAD_SIZE
    ).transpose(1, 0, 2, 3)


def kv_groups(matrix, kv_count):
    return matrix.reshape(matrix.shape[0], kv_count, HEAD_SIZE).transpose(1, 0, 2)


def query_partials(queries, key_rows, value_rows, visible):
    kv_count = key_rows.shape[1] // HEAD_SIZE

    def query_per_head(operands):
        query_part, key_part, value_part = operands
        scores = (
            jnp.einsum("qgd,sd->qgs", query_part, key_part, preferred_element_type=jnp.float32)
            * FACTOR
        )
        shown = visible[:, None, :]
        peak_score = jnp.max(jnp.where(shown, scores, MASKED_SCORE), -1)
        weights = jnp.where(shown, jnp.exp(scores - peak_score[..., None]), 0.0)
        totals = jnp.sum(weights, -1)
        partial_acc = jnp.einsum(
            "qgs,sd->qgd",
            weights.astype(jnp.bfloat16),
            value_part,
            preferred_element_type=jnp.float32,
        )
        return (peak_score, totals, partial_acc)

    peaks, totals, accums = lax.map(
        query_per_head,
        (
            head_groups(queries, kv_count),
            kv_groups(key_rows, kv_count),
            kv_groups(value_rows, kv_count),
        ),
    )
    query_count = queries.shape[0]
    peaks = peaks.transpose(1, 0, 2).reshape(query_count, -1)
    totals = totals.transpose(1, 0, 2).reshape(query_count, -1)
    accums = accums.transpose(1, 0, 2, 3).reshape(query_count, -1)
    return (peaks, totals, accums)


def gathered(context_queries, context_keys, context_values, doc_ids, query_token_rows, span_start):
    host = lax.axis_index("hosts")
    host_count = lax.axis_size("hosts")
    block = context_queries.shape[0]
    per_host = query_token_rows.shape[0]
    kv_count = context_keys.shape[1] // HEAD_SIZE
    anchor = from_root(jnp.stack([context_keys, context_values]), "hosts", 0)
    pieces = [
        anchor[:, :, h * HEAD_SIZE : (h + 1) * HEAD_SIZE].reshape(2 * block, HEAD_SIZE)
        for h in range(kv_count)
    ]
    block_out = context_attention(
        host.reshape(1).astype(jnp.int32),
        jnp.zeros((1,), jnp.int32),
        own_bias(doc_ids.reshape(1, block)),
        context_queries,
        context_keys,
        context_values,
        pieces,
    )
    all_queries, all_spans = (
        lax.all_gather(query_token_rows, "hosts", axis=0, tiled=True),
        lax.all_gather(span_start, "hosts", axis=0, tiled=True),
    )
    key_positions = host * block + jnp.arange(block, dtype=jnp.int32)
    query_visible = key_positions[None, :] >= all_spans[:, None]
    peaks, totals, accums = query_partials(
        all_queries, context_keys, context_values, query_visible
    )
    received = [
        lax.all_to_all(x, "hosts", split_axis=0, concat_axis=0, tiled=True).reshape(
            host_count, per_host, -1
        )
        for x in (peaks, totals, accums)
    ]
    source_peaks, source_totals, source_accums = received
    overall = jnp.max(source_peaks, 0)
    scales = jnp.exp(source_peaks - overall[None])
    own_totals = jnp.sum(scales * source_totals, 0)
    own_accums = jnp.sum(jnp.repeat(scales, HEAD_SIZE, axis=2) * source_accums, 0)
    answer = (own_accums / jnp.repeat(own_totals, HEAD_SIZE, axis=1)).astype(jnp.bfloat16)
    return (block_out, answer)


def solution(mesh):
    rows = P(("groups", "hosts"), "tensor")
    words = P(("groups", "hosts"))

    def on_device(context_queries, context_keys, context_values, doc_ids, query_rows, span_start):
        kv_count = context_keys.shape[1] // HEAD_SIZE
        fits = mesh.shape["hosts"] == 2 * kv_count and kv_count == 4 and query_rows.shape[0] == 1
        plan = paired if fits else gathered
        return plan(
            context_queries, context_keys, context_values, doc_ids, query_rows, span_start
        )

    return jax.shard_map(
        on_device,
        mesh=mesh,
        in_specs=(rows, rows, rows, words, rows, words),
        out_specs=(rows, rows),
        check_vma=False,
    )
```

```python
import functools

import jax
import jax.numpy as jnp
from jax import lax
from jax.experimental import pallas as pl
from jax.experimental.pallas import tpu as pltpu
from jax.sharding import PartitionSpec as P

HEAD_SIZE = 128
MASKED_SCORE = -1e30
FACTOR = float(HEAD_SIZE) ** -0.5
LOG2E = 1.4426950408889634
VMEM = pl.BlockSpec(memory_space=pltpu.VMEM)
SMEM = pl.BlockSpec(memory_space=pltpu.SMEM)
HBM = pl.BlockSpec(memory_space=pltpu.HBM)
SPAN_ROWS = 16
WORD_ROWS = 16
UNIT = 4
NT = (((1,), (1,)), ((), ()))


def in_hbm(x):
    return pltpu.with_memory_space_constraint(x, pltpu.HBM)


def dot_nt(a, b):
    return lax.dot_general(a, b, NT, preferred_element_type=jnp.float32)


def dot_nn(a, b):
    return jnp.dot(a, b, preferred_element_type=jnp.float32)


def span_rows(start):
    row = lax.broadcasted_iota(jnp.int32, (SPAN_ROWS, HEAD_SIZE), 0)
    start = jnp.broadcast_to(start, (SPAN_ROWS, HEAD_SIZE))
    digit = jnp.where(row < SPAN_ROWS // 2, start // HEAD_SIZE, start % HEAD_SIZE)
    return digit.astype(jnp.float32).astype(jnp.bfloat16)


def span_of(rows):
    digits = rows.astype(jnp.float32)
    return digits[0:1, :] * HEAD_SIZE + digits[SPAN_ROWS // 2 : SPAN_ROWS // 2 + 1, :]


def own_bias(doc_row):
    block = doc_row.shape[1]
    row = lax.broadcasted_iota(jnp.int32, (block, block), 0)
    lane = lax.broadcasted_iota(jnp.int32, (block, block), 1)
    along = jnp.broadcast_to(doc_row.astype(jnp.float32), (block, block))
    return jnp.where((lane <= row) & (jnp.transpose(along) == along), 0.0, MASKED_SCORE)


def prepare_kernel(span_ref, *refs):
    sources, (message_ref, bias_ref, *staged), scratch = refs[:5], refs[5:10], refs[10:]
    row, docs, rows_ref, sems = scratch
    heads = row.shape[1] // HEAD_SIZE
    copies = [
        pltpu.make_async_copy(source, target, sems.at[i])
        for i, (source, target) in enumerate(zip(sources, (row, docs, *staged)))
    ]
    for copy in copies:
        copy.start()
    copies[0].wait()
    query = row[...].astype(jnp.float32)
    for head in range(heads):
        rows_ref[head : head + 1, :] = query[:, head * HEAD_SIZE : (head + 1) * HEAD_SIZE]
    message_ref[:heads, :] = rows_ref[...].astype(jnp.bfloat16)
    message_ref[heads:, :] = span_rows(span_ref[...].reshape(1, 1))
    copies[1].wait()
    bias_ref[...] = own_bias(docs[...])
    for copy in copies[2:]:
        copy.wait()


def prepare(span, query_row, docs, keys, values, context_queries):
    heads = query_row.shape[1] // HEAD_SIZE
    block = keys.shape[0]
    staged = (keys, values, context_queries)
    out_shape = [
        pltpu.VMEM((heads + SPAN_ROWS, HEAD_SIZE), query_row.dtype),
        pltpu.VMEM((block, block), jnp.float32),
    ] + [pltpu.VMEM(x.shape, x.dtype) for x in staged]
    return pl.pallas_call(
        prepare_kernel,
        out_shape=out_shape,
        in_specs=[VMEM] + [HBM] * 5,
        out_specs=[VMEM] * len(out_shape),
        scratch_shapes=[
            pltpu.VMEM(query_row.shape, query_row.dtype),
            pltpu.VMEM((1, block), jnp.int32),
            pltpu.VMEM((heads, HEAD_SIZE), jnp.float32),
            pltpu.SemaphoreType.DMA((5,)),
        ],
        compiler_params=pltpu.CompilerParams(vmem_limit_bytes=8 * 2**20),
        cost_estimate=pl.CostEstimate(flops=1000, bytes_accessed=2600000, transcendentals=0),
        name="prepare",
    )(span, *[in_hbm(x) for x in (query_row, docs.reshape(1, block), *staged)])


def partials_kernel(host_ref, k0_ref, v0_ref, k1_ref, v1_ref, *refs):
    message_refs, out_refs = refs[:-2], refs[-2:]
    block = k0_ref.shape[0]
    kv_count = k0_ref.shape[1] // HEAD_SIZE
    heads = message_refs[0].shape[0] - SPAN_ROWS
    per_kv = heads // kv_count
    messages = [ref[...] for ref in message_refs]
    rows = len(messages) * heads
    host = host_ref[0]
    queries = jnp.concatenate([message[:heads] for message in messages], 0)
    starts = jnp.concatenate(
        [
            jnp.broadcast_to(span_of(message[heads:]), (heads, HEAD_SIZE))
            for message in messages
        ],
        0,
    )
    row_kv = (lax.broadcasted_iota(jnp.int32, (rows, HEAD_SIZE), 0) % heads) // per_kv
    lanes = lax.broadcasted_iota(jnp.int32, (rows, block), 1)

    def chosen(per_head):
        out = per_head[0]
        for index in range(1, kv_count):
            out = jnp.where(row_kv == index, per_head[index], out)
        return out

    scores, shown = [], []
    for key_ref, at in ((k0_ref, host), (k1_ref, host ^ 1)):
        scores.append(
            chosen(
                [
                    dot_nt(queries, key_ref[:, h * HEAD_SIZE : (h + 1) * HEAD_SIZE])
                    for h in range(kv_count)
                ]
            )
            * FACTOR
        )
        shown.append((lanes + at * block).astype(jnp.float32) >= starts)
    masked = [jnp.where(s, x, MASKED_SCORE) for s, x in zip(shown, scores)]
    peaks = [jnp.max(x, -1, keepdims=True) for x in masked]
    weights = [
        jnp.where(s, jnp.exp(x - p), 0.0) for s, x, p in zip(shown, masked, peaks)
    ]
    peak = jnp.maximum(peaks[0], peaks[1])
    scales = [jnp.exp(p - peak) for p in peaks]
    total, acc = 0.0, 0.0
    for weight, scale, value_ref in zip(weights, scales, (v0_ref, v1_ref)):
        total += scale * jnp.sum(weight, -1, keepdims=True)
        weight = weight.astype(jnp.bfloat16)
        acc += scale * chosen(
            [
                dot_nn(weight, value_ref[:, h * HEAD_SIZE : (h + 1) * HEAD_SIZE])
                for h in range(kv_count)
            ]
        )
    peak_row = jnp.transpose(jnp.broadcast_to(peak, (rows, rows)))[0:1, :]
    total_row = jnp.transpose(jnp.broadcast_to(total, (rows, rows)))[0:1, :]
    acc = acc.astype(jnp.bfloat16)
    row = lax.broadcasted_iota(jnp.int32, (WORD_ROWS, HEAD_SIZE), 0)
    words = jnp.zeros((WORD_ROWS, HEAD_SIZE), jnp.float32)
    for at, rest in ((0, peak_row), (3, total_row)):
        for digit in range(3):
            part = rest.astype(jnp.bfloat16).astype(jnp.float32)
            words = jnp.where(row == at + digit, part, words)
            rest = rest - part
    words = words.astype(jnp.bfloat16)
    size = message_refs[0].shape[0]
    for index in range(len(messages)):
        out_ref, at = out_refs[index // 2], index % 2 * size
        out_ref[at : at + heads, :] = acc[index * heads : (index + 1) * heads]
        out_ref[at + heads : at + size, :] = words


def partials(host, keys, values, other_keys, other_values, messages):
    rows, width = messages[0].shape
    part = pltpu.VMEM((2 * rows, width), messages[0].dtype)
    return pl.pallas_call(
        partials_kernel,
        out_shape=[part] * 2,
        in_specs=[SMEM] + [VMEM] * (4 + len(messages)),
        out_specs=[VMEM] * 2,
        compiler_params=pltpu.CompilerParams(vmem_limit_bytes=8 * 2**20),
        cost_estimate=pl.CostEstimate(flops=1000000, bytes_accessed=900000, transcendentals=40000),
        name="query_partials",
    )(host, keys, values, other_keys, other_values, *messages)


def merged_answer(parts):
    heads = parts[0][0].shape[0] - WORD_ROWS
    row = lax.broadcasted_iota(jnp.int32, (heads, HEAD_SIZE), 0)
    lane = lax.broadcasted_iota(jnp.int32, (heads, HEAD_SIZE), 1)
    peaks, totals, sums = [], [], []
    for part, index in parts:
        sums.append(part[:heads].astype(jnp.float32))
        words = part[heads:].astype(jnp.float32)
        for at, out in ((0, peaks), (3, totals)):
            word = words[at : at + 1, :] + words[at + 1 : at + 2, :] + words[at + 2 : at + 3, :]
            word = jnp.broadcast_to(word, (heads, HEAD_SIZE))
            picked = jnp.where(lane == row + index * heads, word, 0.0)
            out.append(jnp.sum(picked, -1, keepdims=True))
    peak = functools.reduce(jnp.maximum, peaks)
    scales = [jnp.exp(p - peak) for p in peaks]
    total = functools.reduce(jnp.add, [s * t for s, t in zip(scales, totals)])
    merged = functools.reduce(jnp.add, [s * a for s, a in zip(scales, sums)])
    return (merged / total).astype(parts[0][0].dtype)


def chosen_anchor(host_ref, held_ref, arrived_ref, at):
    columns = slice(at, at + HEAD_SIZE)
    odd = jnp.full((held_ref.shape[0], HEAD_SIZE), (host_ref[0] // 2) % 2, jnp.int32)
    return jnp.where(odd == 0, held_ref[:, columns], arrived_ref[:, columns])


def weights_kernel(host_ref, bias_ref, query_ref, key_ref, held_ref, arrived_ref, out_ref):
    block = query_ref.shape[0]
    kv_count = key_ref.shape[1] // HEAD_SIZE
    group = query_ref.shape[1] // key_ref.shape[1]
    scale = FACTOR * LOG2E
    front = jnp.where(host_ref[0] > 0, 0.0, MASKED_SCORE)
    bias = jnp.concatenate([bias_ref[...], jnp.full((block, block), front, jnp.float32)], 1)
    bias = jnp.concatenate([bias] * UNIT, 0)

    def score(first):
        at = first // group * HEAD_SIZE
        far = chosen_anchor(host_ref, held_ref, arrived_ref, at)
        keys = jnp.concatenate([key_ref[:, at : at + HEAD_SIZE], far], 0)
        query = jnp.concatenate(
            [
                query_ref[:, (first + i) * HEAD_SIZE : (first + i + 1) * HEAD_SIZE]
                for i in range(UNIT)
            ],
            0,
        )
        return dot_nt(query, keys)

    def weigh(first, scores):
        scores = scores + bias
        peak = jnp.max(scores, -1, keepdims=True)
        weights = jnp.exp2((scores - peak) * scale)
        out_ref[first * block : (first + UNIT) * block, :] = weights.astype(jnp.bfloat16)

    waiting = None
    for first in range(0, kv_count * group, UNIT):
        scores = score(first)
        if waiting is not None:
            weigh(*waiting)
        waiting = (first, scores)
    weigh(*waiting)


def context_weights(host, bias, queries, keys, held, arrived):
    block, width = queries.shape
    heads = width // HEAD_SIZE
    return pl.pallas_call(
        weights_kernel,
        out_shape=pltpu.VMEM((heads * block, 2 * block), queries.dtype),
        in_specs=[SMEM] + [VMEM] * 5,
        out_specs=VMEM,
        compiler_params=pltpu.CompilerParams(vmem_limit_bytes=16 * 2**20),
        cost_estimate=pl.CostEstimate(
            flops=4 * block * block * width,
            bytes_accessed=4000000,
            transcendentals=2 * heads * block * block,
        ),
        name="context_weights",
    )(host, bias, queries, keys, held, arrived)


def load_kernel(held_ref, kept_ref, back_ref, out_ref):
    block, kv_count = held_ref.shape[0], held_ref.shape[1] // HEAD_SIZE
    size = kept_ref.shape[0] // 2
    for head in range(kv_count):
        columns = slice(head * HEAD_SIZE, (head + 1) * HEAD_SIZE)
        out_ref[head * block : (head + 1) * block, :] = held_ref[:, columns]
    rest = kv_count * block
    out_ref[rest : rest + size, :] = kept_ref[size:, :]
    out_ref[rest + size :, :] = back_ref[size:, :]


def load(held, kept, back):
    rows = held.size // HEAD_SIZE + kept.shape[0]
    return pl.pallas_call(
        load_kernel,
        out_shape=pltpu.VMEM((rows, HEAD_SIZE), held.dtype),
        in_specs=[VMEM] * 3,
        out_specs=VMEM,
        compiler_params=pltpu.CompilerParams(vmem_limit_bytes=8 * 2**20),
        cost_estimate=pl.CostEstimate(flops=1000, bytes_accessed=300000, transcendentals=0),
        name="load",
    )(held, kept, back)


def sums_kernel(answers, host_ref, weight_ref, value_ref, held_ref, arrived_ref, *refs):
    part_refs, scratch = refs[: len(refs) - 4 - answers], refs[-3:]
    out_ref, *answer_refs = refs[len(part_refs) : -3]
    slabs, row, sems = scratch
    kv_count, block, slab = slabs.shape
    group = slab // HEAD_SIZE
    ones = jnp.ones((2 * block, HEAD_SIZE), jnp.bfloat16)
    copies, waiting = [], None
    for answer_ref in answer_refs:
        kept_ref, back_ref = part_refs
        size, rest = kept_ref.shape[0] // 2, kv_count * block
        answer = merged_answer(
            [
                (kept_ref[:size, :], 0),
                (arrived_ref[rest : rest + size, :], 1),
                (back_ref[:size, :], 2),
                (arrived_ref[rest + size :, :], 3),
            ]
        )
        for head in range(answer.shape[0]):
            row[:, head * HEAD_SIZE : (head + 1) * HEAD_SIZE] = answer[head : head + 1, :]
        copies.append(pltpu.make_async_copy(row, answer_ref, sems.at[kv_count]))
        copies[-1].start()

    odd = jnp.full((block, HEAD_SIZE), (host_ref[0] // 2) % 2, jnp.int32)

    def add(first):
        index = first // group
        rows = slice(index * block, (index + 1) * block)
        far = jnp.where(odd == 0, held_ref[rows, :], arrived_ref[rows, :])
        near = value_ref[:, index * HEAD_SIZE : (index + 1) * HEAD_SIZE]
        values = jnp.concatenate([near, far], 0)
        weights = weight_ref[first * block : (first + UNIT) * block, :]
        return dot_nn(weights, jnp.concatenate([values, ones], 1))

    def finish(first, sums):
        total = sums[:, HEAD_SIZE:]
        inverse = pl.reciprocal(total, approx=True)
        inverse = inverse * (2.0 - total * inverse)
        out = (sums[:, :HEAD_SIZE] * inverse).astype(jnp.bfloat16)
        index = first // group
        for i in range(UNIT):
            column = (first % group + i) * HEAD_SIZE
            slabs[index, :, column : column + HEAD_SIZE] = out[i * block : (i + 1) * block, :]
        if first % group + UNIT == group:
            copy = pltpu.make_async_copy(
                slabs.at[index], out_ref.at[:, pl.ds(index * slab, slab)], sems.at[index]
            )
            copy.start()
            copies.append(copy)

    for first in range(0, kv_count * group, UNIT):
        sums = add(first)
        if waiting is not None:
            finish(*waiting)
        waiting = (first, sums)
    finish(*waiting)
    for copy in copies:
        copy.wait()


def context_sums(host, weights, values, held, arrived, parts):
    block, kv_count = values.shape[0], values.shape[1] // HEAD_SIZE
    width = weights.shape[0] // block * HEAD_SIZE
    answers = 1 if parts else 0
    return pl.pallas_call(
        functools.partial(sums_kernel, answers),
        out_shape=[jax.ShapeDtypeStruct((block, width), values.dtype)]
        + [jax.ShapeDtypeStruct((1, width), values.dtype)] * answers,
        in_specs=[SMEM] + [VMEM] * (4 + len(parts)),
        out_specs=[HBM] * (1 + answers),
        scratch_shapes=[
            pltpu.VMEM((kv_count, block, width // kv_count), values.dtype),
            pltpu.VMEM((1, width), values.dtype),
            pltpu.SemaphoreType.DMA((kv_count + 1,)),
        ],
        compiler_params=pltpu.CompilerParams(vmem_limit_bytes=16 * 2**20),
        cost_estimate=pl.CostEstimate(
            flops=4 * block * block * width, bytes_accessed=4000000, transcendentals=0
        ),
        name="context_sums",
    )(host, weights, values, held, arrived, *parts)


def paired(context_queries, context_keys, context_values, doc_ids, query_token_rows, span_start):
    host_count = lax.axis_size("hosts")
    host = lax.axis_index("hosts")
    place, side = host // 2, host % 2

    def swap(value, mask):
        return lax.ppermute(value, "hosts", [(i, i ^ mask) for i in range(host_count)])

    def down(value):
        return lax.ppermute(value, "hosts", [(x, 4 + x) for x in (0, 1)])

    other_keys, other_values = swap(context_keys, 1), swap(context_values, 1)
    message, bias, keys, values, queries = prepare(
        span_start, query_token_rows, doc_ids, context_keys, context_values, context_queries
    )

    def descend(own, other):
        first = jnp.where(side == 0, own, other)
        return jnp.where(place == 2, down(first), first)

    messages = [message] + [swap(message, 2 * k) for k in (1, 2, 3)]
    held_keys = descend(keys, other_keys)
    arrived_keys = swap(held_keys, 2)
    host_word = host.reshape(1).astype(jnp.int32)
    kept, sent = partials(host_word, keys, values, other_keys, other_values, messages)
    back = swap(sent, 4)
    loaded = load(descend(values, other_values), kept, back)
    arrived = swap(loaded, 2)
    weights = context_weights(host_word, bias, queries, keys, held_keys, arrived_keys)
    return tuple(context_sums(host_word, weights, values, loaded, arrived, [kept, back]))


def from_root(value, axis, source):
    kept = jnp.where(lax.axis_index(axis) == source, value, 0).astype(value.dtype)
    return lax.psum(kept, axis)


def head_groups(matrix, kv_count):
    count_rows = matrix.shape[0]
    return matrix.reshape(
        count_rows, kv_count, matrix.shape[1] // (kv_count * HEAD_SIZE), HEAD_SIZE
    ).transpose(1, 0, 2, 3)


def kv_groups(matrix, kv_count):
    return matrix.reshape(matrix.shape[0], kv_count, HEAD_SIZE).transpose(1, 0, 2)


def query_partials(queries, key_rows, value_rows, visible):
    kv_count = key_rows.shape[1] // HEAD_SIZE

    def query_per_head(operands):
        query_part, key_part, value_part = operands
        scores = (
            jnp.einsum("qgd,sd->qgs", query_part, key_part, preferred_element_type=jnp.float32)
            * FACTOR
        )
        shown = visible[:, None, :]
        peak_score = jnp.max(jnp.where(shown, scores, MASKED_SCORE), -1)
        weights = jnp.where(shown, jnp.exp(scores - peak_score[..., None]), 0.0)
        totals = jnp.sum(weights, -1)
        partial_acc = jnp.einsum(
            "qgs,sd->qgd",
            weights.astype(jnp.bfloat16),
            value_part,
            preferred_element_type=jnp.float32,
        )
        return (peak_score, totals, partial_acc)

    peaks, totals, accums = lax.map(
        query_per_head,
        (
            head_groups(queries, kv_count),
            kv_groups(key_rows, kv_count),
            kv_groups(value_rows, kv_count),
        ),
    )
    query_count = queries.shape[0]
    peaks = peaks.transpose(1, 0, 2).reshape(query_count, -1)
    totals = totals.transpose(1, 0, 2).reshape(query_count, -1)
    accums = accums.transpose(1, 0, 2, 3).reshape(query_count, -1)
    return (peaks, totals, accums)


def gathered(context_queries, context_keys, context_values, doc_ids, query_token_rows, span_start):
    host = lax.axis_index("hosts")
    host_count = lax.axis_size("hosts")
    block = context_queries.shape[0]
    per_host = query_token_rows.shape[0]
    anchor = from_root(jnp.stack([context_keys, context_values]), "hosts", 0)
    weights = context_weights(
        host.reshape(1).astype(jnp.int32),
        own_bias(doc_ids.reshape(1, block)),
        context_queries,
        context_keys,
        anchor[0],
        anchor[0],
    )
    kv_count = context_keys.shape[1] // HEAD_SIZE
    by_head = anchor[1].reshape(block, kv_count, HEAD_SIZE).transpose(1, 0, 2)
    by_head = by_head.reshape(kv_count * block, HEAD_SIZE)
    (block_out,) = context_sums(
        host.reshape(1).astype(jnp.int32), weights, context_values, by_head, by_head, []
    )
    all_queries, all_spans = (
        lax.all_gather(query_token_rows, "hosts", axis=0, tiled=True),
        lax.all_gather(span_start, "hosts", axis=0, tiled=True),
    )
    key_positions = host * block + jnp.arange(block, dtype=jnp.int32)
    query_visible = key_positions[None, :] >= all_spans[:, None]
    peaks, totals, accums = query_partials(
        all_queries, context_keys, context_values, query_visible
    )
    received = [
        lax.all_to_all(x, "hosts", split_axis=0, concat_axis=0, tiled=True).reshape(
            host_count, per_host, -1
        )
        for x in (peaks, totals, accums)
    ]
    source_peaks, source_totals, source_accums = received
    overall = jnp.max(source_peaks, 0)
    scales = jnp.exp(source_peaks - overall[None])
    own_totals = jnp.sum(scales * source_totals, 0)
    own_accums = jnp.sum(jnp.repeat(scales, HEAD_SIZE, axis=2) * source_accums, 0)
    answer = (own_accums / jnp.repeat(own_totals, HEAD_SIZE, axis=1)).astype(jnp.bfloat16)
    return (block_out, answer)


def solution(mesh):
    rows = P(("groups", "hosts"), "tensor")
    words = P(("groups", "hosts"))

    def on_device(context_queries, context_keys, context_values, doc_ids, query_rows, span_start):
        kv_count = context_keys.shape[1] // HEAD_SIZE
        fits = mesh.shape["hosts"] == 2 * kv_count and kv_count == 4 and query_rows.shape[0] == 1
        plan = paired if fits else gathered
        return plan(
            context_queries, context_keys, context_values, doc_ids, query_rows, span_start
        )

    return jax.shard_map(
        on_device,
        mesh=mesh,
        in_specs=(rows, rows, rows, words, rows, words),
        out_specs=(rows, rows),
        check_vma=False,
    )
```

```python
import functools

import jax
import jax.numpy as jnp
from jax import lax
from jax.experimental import pallas as pl
from jax.experimental.pallas import tpu as pltpu
from jax.sharding import PartitionSpec as P

HEAD_SIZE = 128
MASKED_SCORE = -1e30
FACTOR = float(HEAD_SIZE) ** -0.5
LOG2E = 1.4426950408889634
VMEM = pl.BlockSpec(memory_space=pltpu.VMEM)
SMEM = pl.BlockSpec(memory_space=pltpu.SMEM)
HBM = pl.BlockSpec(memory_space=pltpu.HBM)
SPAN_ROWS = 16
WORD_ROWS = 16
UNIT = 4
NT = (((1,), (1,)), ((), ()))


def in_hbm(x):
    return pltpu.with_memory_space_constraint(x, pltpu.HBM)


def dot_nt(a, b):
    return lax.dot_general(a, b, NT, preferred_element_type=jnp.float32)


def dot_nn(a, b):
    return jnp.dot(a, b, preferred_element_type=jnp.float32)


def span_rows(start):
    row = lax.broadcasted_iota(jnp.int32, (SPAN_ROWS, HEAD_SIZE), 0)
    start = jnp.broadcast_to(start, (SPAN_ROWS, HEAD_SIZE))
    digit = jnp.where(row < SPAN_ROWS // 2, start // HEAD_SIZE, start % HEAD_SIZE)
    return digit.astype(jnp.float32).astype(jnp.bfloat16)


def span_of(rows):
    digits = rows.astype(jnp.float32)
    return digits[0:1, :] * HEAD_SIZE + digits[SPAN_ROWS // 2 : SPAN_ROWS // 2 + 1, :]


def own_bias(doc_row):
    block = doc_row.shape[1]
    row = lax.broadcasted_iota(jnp.int32, (block, block), 0)
    lane = lax.broadcasted_iota(jnp.int32, (block, block), 1)
    along = jnp.broadcast_to(doc_row.astype(jnp.float32), (block, block))
    return jnp.where((lane <= row) & (jnp.transpose(along) == along), 0.0, MASKED_SCORE)


def prepare_kernel(span_ref, *refs):
    sources, (message_ref, *staged), (row, rows_ref, sems) = refs[:3], refs[3:6], refs[6:]
    heads = row.shape[1] // HEAD_SIZE
    copies = [
        pltpu.make_async_copy(source, target, sems.at[i])
        for i, (source, target) in enumerate(zip(sources, (row, *staged)))
    ]
    for copy in copies:
        copy.start()
    copies[0].wait()
    query = row[...].astype(jnp.float32)
    for head in range(heads):
        rows_ref[head : head + 1, :] = query[:, head * HEAD_SIZE : (head + 1) * HEAD_SIZE]
    message_ref[:heads, :] = rows_ref[...].astype(jnp.bfloat16)
    message_ref[heads:, :] = span_rows(span_ref[...].reshape(1, 1))
    for copy in copies[1:]:
        copy.wait()


def prepare(span, query_row, keys, values):
    heads = query_row.shape[1] // HEAD_SIZE
    out_shape = [pltpu.VMEM((heads + SPAN_ROWS, HEAD_SIZE), query_row.dtype)]
    out_shape += [pltpu.VMEM(x.shape, x.dtype) for x in (keys, values)]
    return pl.pallas_call(
        prepare_kernel,
        out_shape=out_shape,
        in_specs=[VMEM] + [HBM] * 3,
        out_specs=[VMEM] * len(out_shape),
        scratch_shapes=[
            pltpu.VMEM(query_row.shape, query_row.dtype),
            pltpu.VMEM((heads, HEAD_SIZE), jnp.float32),
            pltpu.SemaphoreType.DMA((3,)),
        ],
        compiler_params=pltpu.CompilerParams(vmem_limit_bytes=8 * 2**20),
        cost_estimate=pl.CostEstimate(flops=1000, bytes_accessed=600000, transcendentals=0),
        name="prepare",
    )(span, *[in_hbm(x) for x in (query_row, keys, values)])


def stage_kernel(docs_ref, query_ref, bias_ref, staged_ref, docs, sems):
    copies = [
        pltpu.make_async_copy(docs_ref, docs, sems.at[0]),
        pltpu.make_async_copy(query_ref, staged_ref, sems.at[1]),
    ]
    for copy in copies:
        copy.start()
    copies[0].wait()
    bias_ref[...] = own_bias(docs[...])
    copies[1].wait()


def stage(docs, context_queries):
    block = docs.shape[0]
    return pl.pallas_call(
        stage_kernel,
        out_shape=[
            pltpu.VMEM((block, block), jnp.float32),
            pltpu.VMEM(context_queries.shape, context_queries.dtype),
        ],
        in_specs=[HBM] * 2,
        out_specs=[VMEM] * 2,
        scratch_shapes=[pltpu.VMEM((1, block), jnp.int32), pltpu.SemaphoreType.DMA((2,))],
        compiler_params=pltpu.CompilerParams(vmem_limit_bytes=8 * 2**20),
        cost_estimate=pl.CostEstimate(flops=1000, bytes_accessed=2100000, transcendentals=0),
        name="stage",
    )(in_hbm(docs.reshape(1, block)), in_hbm(context_queries))


def partials_kernel(host_ref, k0_ref, v0_ref, k1_ref, v1_ref, *refs):
    message_refs, out_refs = refs[:-2], refs[-2:]
    block = k0_ref.shape[0]
    kv_count = k0_ref.shape[1] // HEAD_SIZE
    heads = message_refs[0].shape[0] - SPAN_ROWS
    per_kv = heads // kv_count
    messages = [message_refs[i][...] for i in (0, 3, 2, 1)]
    rows = len(messages) * heads
    host = host_ref[0]
    queries = jnp.concatenate([message[:heads] for message in messages], 0)
    starts = jnp.concatenate(
        [
            jnp.broadcast_to(span_of(message[heads:]), (heads, HEAD_SIZE))
            for message in messages
        ],
        0,
    )
    row_kv = (lax.broadcasted_iota(jnp.int32, (rows, HEAD_SIZE), 0) % heads) // per_kv
    lanes = lax.broadcasted_iota(jnp.int32, (rows, block), 1)

    def chosen(per_head):
        out = per_head[0]
        for index in range(1, kv_count):
            out = jnp.where(row_kv == index, per_head[index], out)
        return out

    scores, shown = [], []
    for key_ref, at in ((k0_ref, host), (k1_ref, host ^ 1)):
        scores.append(
            chosen(
                [
                    dot_nt(queries, key_ref[:, h * HEAD_SIZE : (h + 1) * HEAD_SIZE])
                    for h in range(kv_count)
                ]
            )
            * FACTOR
        )
        shown.append((lanes + at * block).astype(jnp.float32) >= starts)
    masked = [jnp.where(s, x, MASKED_SCORE) for s, x in zip(shown, scores)]
    peaks = [jnp.max(x, -1, keepdims=True) for x in masked]
    weights = [
        jnp.where(s, jnp.exp(x - p), 0.0) for s, x, p in zip(shown, masked, peaks)
    ]
    peak = jnp.maximum(peaks[0], peaks[1])
    scales = [jnp.exp(p - peak) for p in peaks]
    total, acc = 0.0, 0.0
    for weight, scale, value_ref in zip(weights, scales, (v0_ref, v1_ref)):
        total += scale * jnp.sum(weight, -1, keepdims=True)
        weight = weight.astype(jnp.bfloat16)
        acc += scale * chosen(
            [
                dot_nn(weight, value_ref[:, h * HEAD_SIZE : (h + 1) * HEAD_SIZE])
                for h in range(kv_count)
            ]
        )
    peak_row = jnp.transpose(jnp.broadcast_to(peak, (rows, rows)))[0:1, :]
    total_row = jnp.transpose(jnp.broadcast_to(total, (rows, rows)))[0:1, :]
    acc = acc.astype(jnp.bfloat16)
    row = lax.broadcasted_iota(jnp.int32, (WORD_ROWS, HEAD_SIZE), 0)
    words = jnp.zeros((WORD_ROWS, HEAD_SIZE), jnp.float32)
    for at, rest in ((0, peak_row), (3, total_row)):
        for digit in range(3):
            part = rest.astype(jnp.bfloat16).astype(jnp.float32)
            words = jnp.where(row == at + digit, part, words)
            rest = rest - part
    words = words.astype(jnp.bfloat16)
    size = message_refs[0].shape[0]
    for index in range(len(messages)):
        out_ref, at = out_refs[index // 2], index % 2 * size
        out_ref[at : at + heads, :] = acc[index * heads : (index + 1) * heads]
        out_ref[at + heads : at + size, :] = words


def partials(host, keys, values, other_keys, other_values, messages):
    rows, width = messages[0].shape
    part = pltpu.VMEM((2 * rows, width), messages[0].dtype)
    return pl.pallas_call(
        partials_kernel,
        out_shape=[part] * 2,
        in_specs=[SMEM] + [VMEM] * (4 + len(messages)),
        out_specs=[VMEM] * 2,
        compiler_params=pltpu.CompilerParams(vmem_limit_bytes=8 * 2**20),
        cost_estimate=pl.CostEstimate(flops=1000000, bytes_accessed=900000, transcendentals=40000),
        name="query_partials",
    )(host, keys, values, other_keys, other_values, *messages)


def merged_answer(parts):
    heads = parts[0][0].shape[0] - WORD_ROWS
    row = lax.broadcasted_iota(jnp.int32, (heads, HEAD_SIZE), 0)
    lane = lax.broadcasted_iota(jnp.int32, (heads, HEAD_SIZE), 1)
    peaks, totals, sums = [], [], []
    for part, index in parts:
        sums.append(part[:heads].astype(jnp.float32))
        words = part[heads:].astype(jnp.float32)
        for at, out in ((0, peaks), (3, totals)):
            word = words[at : at + 1, :] + words[at + 1 : at + 2, :] + words[at + 2 : at + 3, :]
            word = jnp.broadcast_to(word, (heads, HEAD_SIZE))
            picked = jnp.where(lane == row + index * heads, word, 0.0)
            out.append(jnp.sum(picked, -1, keepdims=True))
    peak = functools.reduce(jnp.maximum, peaks)
    scales = [jnp.exp(p - peak) for p in peaks]
    total = functools.reduce(jnp.add, [s * t for s, t in zip(scales, totals)])
    merged = functools.reduce(jnp.add, [s * a for s, a in zip(scales, sums)])
    return (merged / total).astype(parts[0][0].dtype)


def chosen_anchor(host_ref, held_ref, arrived_ref, at):
    columns = slice(at, at + HEAD_SIZE)
    odd = jnp.full((held_ref.shape[0], HEAD_SIZE), (host_ref[0] // 2) % 2, jnp.int32)
    return jnp.where(odd == 0, held_ref[:, columns], arrived_ref[:, columns])


def weights_kernel(host_ref, bias_ref, query_ref, key_ref, held_ref, arrived_ref, out_ref):
    block = query_ref.shape[0]
    kv_count = key_ref.shape[1] // HEAD_SIZE
    group = query_ref.shape[1] // key_ref.shape[1]
    scale = FACTOR * LOG2E
    front = jnp.where(host_ref[0] > 0, 0.0, MASKED_SCORE)
    bias = jnp.concatenate([bias_ref[...], jnp.full((block, block), front, jnp.float32)], 1)
    bias = jnp.concatenate([bias] * UNIT, 0)

    def score(first):
        at = first // group * HEAD_SIZE
        far = chosen_anchor(host_ref, held_ref, arrived_ref, at)
        keys = jnp.concatenate([key_ref[:, at : at + HEAD_SIZE], far], 0)
        query = jnp.concatenate(
            [
                query_ref[:, (first + i) * HEAD_SIZE : (first + i + 1) * HEAD_SIZE]
                for i in range(UNIT)
            ],
            0,
        )
        return dot_nt(query, keys)

    def weigh(first, scores):
        scores = scores + bias
        peak = jnp.max(scores, -1, keepdims=True)
        weights = jnp.exp2((scores - peak) * scale)
        out_ref[first * block : (first + UNIT) * block, :] = weights.astype(jnp.bfloat16)

    waiting = None
    for first in range(0, kv_count * group, UNIT):
        scores = score(first)
        if waiting is not None:
            weigh(*waiting)
        waiting = (first, scores)
    weigh(*waiting)


def context_weights(host, bias, queries, keys, held, arrived):
    block, width = queries.shape
    heads = width // HEAD_SIZE
    return pl.pallas_call(
        weights_kernel,
        out_shape=pltpu.VMEM((heads * block, 2 * block), queries.dtype),
        in_specs=[SMEM] + [VMEM] * 5,
        out_specs=VMEM,
        compiler_params=pltpu.CompilerParams(vmem_limit_bytes=16 * 2**20),
        cost_estimate=pl.CostEstimate(
            flops=4 * block * block * width,
            bytes_accessed=4000000,
            transcendentals=2 * heads * block * block,
        ),
        name="context_weights",
    )(host, bias, queries, keys, held, arrived)


def load_kernel(held_ref, kept_ref, back_ref, out_ref):
    block, kv_count = held_ref.shape[0], held_ref.shape[1] // HEAD_SIZE
    size = kept_ref.shape[0] // 2
    for head in range(kv_count):
        columns = slice(head * HEAD_SIZE, (head + 1) * HEAD_SIZE)
        out_ref[head * block : (head + 1) * block, :] = held_ref[:, columns]
    rest = kv_count * block
    out_ref[rest : rest + size, :] = kept_ref[size:, :]
    out_ref[rest + size :, :] = back_ref[size:, :]


def load(held, kept, back):
    rows = held.size // HEAD_SIZE + kept.shape[0]
    return pl.pallas_call(
        load_kernel,
        out_shape=pltpu.VMEM((rows, HEAD_SIZE), held.dtype),
        in_specs=[VMEM] * 3,
        out_specs=VMEM,
        compiler_params=pltpu.CompilerParams(vmem_limit_bytes=8 * 2**20),
        cost_estimate=pl.CostEstimate(flops=1000, bytes_accessed=300000, transcendentals=0),
        name="load",
    )(held, kept, back)


def sums_kernel(answers, host_ref, weight_ref, value_ref, held_ref, arrived_ref, *refs):
    part_refs, scratch = refs[: len(refs) - 4 - answers], refs[-3:]
    out_ref, *answer_refs = refs[len(part_refs) : -3]
    slabs, row, sems = scratch
    kv_count, block, slab = slabs.shape
    group = slab // HEAD_SIZE
    ones = jnp.ones((2 * block, HEAD_SIZE), jnp.bfloat16)
    copies, waiting = [], None
    for answer_ref in answer_refs:
        kept_ref, back_ref = part_refs
        size, rest = kept_ref.shape[0] // 2, kv_count * block
        answer = merged_answer(
            [
                (kept_ref[:size, :], 0),
                (arrived_ref[rest : rest + size, :], 1),
                (back_ref[:size, :], 2),
                (arrived_ref[rest + size :, :], 3),
            ]
        )
        for head in range(answer.shape[0]):
            row[:, head * HEAD_SIZE : (head + 1) * HEAD_SIZE] = answer[head : head + 1, :]
        copies.append(pltpu.make_async_copy(row, answer_ref, sems.at[kv_count]))
        copies[-1].start()

    odd = jnp.full((block, HEAD_SIZE), (host_ref[0] // 2) % 2, jnp.int32)

    def add(first):
        index = first // group
        rows = slice(index * block, (index + 1) * block)
        far = jnp.where(odd == 0, held_ref[rows, :], arrived_ref[rows, :])
        near = value_ref[:, index * HEAD_SIZE : (index + 1) * HEAD_SIZE]
        values = jnp.concatenate([near, far], 0)
        weights = weight_ref[first * block : (first + UNIT) * block, :]
        return dot_nn(weights, jnp.concatenate([values, ones], 1))

    def finish(first, sums):
        total = sums[:, HEAD_SIZE:]
        inverse = pl.reciprocal(total, approx=True)
        inverse = inverse * (2.0 - total * inverse)
        out = (sums[:, :HEAD_SIZE] * inverse).astype(jnp.bfloat16)
        index = first // group
        for i in range(UNIT):
            column = (first % group + i) * HEAD_SIZE
            slabs[index, :, column : column + HEAD_SIZE] = out[i * block : (i + 1) * block, :]
        if first % group + UNIT == group:
            copy = pltpu.make_async_copy(
                slabs.at[index], out_ref.at[:, pl.ds(index * slab, slab)], sems.at[index]
            )
            copy.start()
            copies.append(copy)

    for first in range(0, kv_count * group, UNIT):
        sums = add(first)
        if waiting is not None:
            finish(*waiting)
        waiting = (first, sums)
    finish(*waiting)
    for copy in copies:
        copy.wait()


def context_sums(host, weights, values, held, arrived, parts):
    block, kv_count = values.shape[0], values.shape[1] // HEAD_SIZE
    width = weights.shape[0] // block * HEAD_SIZE
    answers = 1 if parts else 0
    return pl.pallas_call(
        functools.partial(sums_kernel, answers),
        out_shape=[jax.ShapeDtypeStruct((block, width), values.dtype)]
        + [jax.ShapeDtypeStruct((1, width), values.dtype)] * answers,
        in_specs=[SMEM] + [VMEM] * (4 + len(parts)),
        out_specs=[HBM] * (1 + answers),
        scratch_shapes=[
            pltpu.VMEM((kv_count, block, width // kv_count), values.dtype),
            pltpu.VMEM((1, width), values.dtype),
            pltpu.SemaphoreType.DMA((kv_count + 1,)),
        ],
        compiler_params=pltpu.CompilerParams(vmem_limit_bytes=16 * 2**20),
        cost_estimate=pl.CostEstimate(
            flops=4 * block * block * width, bytes_accessed=4000000, transcendentals=0
        ),
        name="context_sums",
    )(host, weights, values, held, arrived, *parts)


def paired(context_queries, context_keys, context_values, doc_ids, query_token_rows, span_start):
    host_count = lax.axis_size("hosts")
    host = lax.axis_index("hosts")
    place, side = host // 2, host % 2

    def swap(value, mask):
        return lax.ppermute(value, "hosts", [(i, i ^ mask) for i in range(host_count)])

    def down(value):
        return lax.ppermute(
            value, "hosts", [(i, i ^ (1 if i // 2 % 2 else 4)) for i in range(host_count)]
        )

    other_keys, other_values = swap(context_keys, 1), swap(context_values, 1)
    message, keys, values = prepare(
        span_start, query_token_rows, context_keys, context_values
    )
    bias, queries = stage(doc_ids, context_queries)

    def descend(own, other):
        first = jnp.where(side == 0, own, other)
        return jnp.where(place == 2, down(first), first)

    messages = [message] + [swap(message, 2 * k) for k in (3, 2, 1)]
    held_keys = descend(keys, other_keys)
    arrived_keys = swap(held_keys, 2)
    host_word = host.reshape(1).astype(jnp.int32)
    kept, sent = partials(host_word, keys, values, other_keys, other_values, messages)
    back = swap(sent, 4)
    loaded = load(descend(values, other_values), kept, back)
    arrived = swap(loaded, 2)
    weights = context_weights(host_word, bias, queries, keys, held_keys, arrived_keys)
    return tuple(context_sums(host_word, weights, values, loaded, arrived, [kept, back]))


def from_root(value, axis, source):
    kept = jnp.where(lax.axis_index(axis) == source, value, 0).astype(value.dtype)
    return lax.psum(kept, axis)


def head_groups(matrix, kv_count):
    count_rows = matrix.shape[0]
    return matrix.reshape(
        count_rows, kv_count, matrix.shape[1] // (kv_count * HEAD_SIZE), HEAD_SIZE
    ).transpose(1, 0, 2, 3)


def kv_groups(matrix, kv_count):
    return matrix.reshape(matrix.shape[0], kv_count, HEAD_SIZE).transpose(1, 0, 2)


def query_partials(queries, key_rows, value_rows, visible):
    kv_count = key_rows.shape[1] // HEAD_SIZE

    def query_per_head(operands):
        query_part, key_part, value_part = operands
        scores = (
            jnp.einsum("qgd,sd->qgs", query_part, key_part, preferred_element_type=jnp.float32)
            * FACTOR
        )
        shown = visible[:, None, :]
        peak_score = jnp.max(jnp.where(shown, scores, MASKED_SCORE), -1)
        weights = jnp.where(shown, jnp.exp(scores - peak_score[..., None]), 0.0)
        totals = jnp.sum(weights, -1)
        partial_acc = jnp.einsum(
            "qgs,sd->qgd",
            weights.astype(jnp.bfloat16),
            value_part,
            preferred_element_type=jnp.float32,
        )
        return (peak_score, totals, partial_acc)

    peaks, totals, accums = lax.map(
        query_per_head,
        (
            head_groups(queries, kv_count),
            kv_groups(key_rows, kv_count),
            kv_groups(value_rows, kv_count),
        ),
    )
    query_count = queries.shape[0]
    peaks = peaks.transpose(1, 0, 2).reshape(query_count, -1)
    totals = totals.transpose(1, 0, 2).reshape(query_count, -1)
    accums = accums.transpose(1, 0, 2, 3).reshape(query_count, -1)
    return (peaks, totals, accums)


def gathered(context_queries, context_keys, context_values, doc_ids, query_token_rows, span_start):
    host = lax.axis_index("hosts")
    host_count = lax.axis_size("hosts")
    block = context_queries.shape[0]
    per_host = query_token_rows.shape[0]
    anchor = from_root(jnp.stack([context_keys, context_values]), "hosts", 0)
    weights = context_weights(
        host.reshape(1).astype(jnp.int32),
        own_bias(doc_ids.reshape(1, block)),
        context_queries,
        context_keys,
        anchor[0],
        anchor[0],
    )
    kv_count = context_keys.shape[1] // HEAD_SIZE
    by_head = anchor[1].reshape(block, kv_count, HEAD_SIZE).transpose(1, 0, 2)
    by_head = by_head.reshape(kv_count * block, HEAD_SIZE)
    (block_out,) = context_sums(
        host.reshape(1).astype(jnp.int32), weights, context_values, by_head, by_head, []
    )
    all_queries, all_spans = (
        lax.all_gather(query_token_rows, "hosts", axis=0, tiled=True),
        lax.all_gather(span_start, "hosts", axis=0, tiled=True),
    )
    key_positions = host * block + jnp.arange(block, dtype=jnp.int32)
    query_visible = key_positions[None, :] >= all_spans[:, None]
    peaks, totals, accums = query_partials(
        all_queries, context_keys, context_values, query_visible
    )
    received = [
        lax.all_to_all(x, "hosts", split_axis=0, concat_axis=0, tiled=True).reshape(
            host_count, per_host, -1
        )
        for x in (peaks, totals, accums)
    ]
    source_peaks, source_totals, source_accums = received
    overall = jnp.max(source_peaks, 0)
    scales = jnp.exp(source_peaks - overall[None])
    own_totals = jnp.sum(scales * source_totals, 0)
    own_accums = jnp.sum(jnp.repeat(scales, HEAD_SIZE, axis=2) * source_accums, 0)
    answer = (own_accums / jnp.repeat(own_totals, HEAD_SIZE, axis=1)).astype(jnp.bfloat16)
    return (block_out, answer)


def solution(mesh):
    rows = P(("groups", "hosts"), "tensor")
    words = P(("groups", "hosts"))

    def on_device(context_queries, context_keys, context_values, doc_ids, query_rows, span_start):
        kv_count = context_keys.shape[1] // HEAD_SIZE
        fits = mesh.shape["hosts"] == 2 * kv_count and kv_count == 4 and query_rows.shape[0] == 1
        plan = paired if fits else gathered
        return plan(
            context_queries, context_keys, context_values, doc_ids, query_rows, span_start
        )

    return jax.shard_map(
        on_device,
        mesh=mesh,
        in_specs=(rows, rows, rows, words, rows, words),
        out_specs=(rows, rows),
        check_vma=False,
    )
```

```python
import functools

import jax
import jax.numpy as jnp
from jax import lax
from jax.experimental import pallas as pl
from jax.experimental.pallas import tpu as pltpu
from jax.sharding import PartitionSpec as P

HEAD_SIZE = 128
MASKED_SCORE = -1e30
FACTOR = float(HEAD_SIZE) ** -0.5
LOG2E = 1.4426950408889634
VMEM = pl.BlockSpec(memory_space=pltpu.VMEM)
SMEM = pl.BlockSpec(memory_space=pltpu.SMEM)
HBM = pl.BlockSpec(memory_space=pltpu.HBM)
SPAN_ROWS = 16
WORD_ROWS = 16
UNIT = 4
NT = (((1,), (1,)), ((), ()))


def in_hbm(x):
    return pltpu.with_memory_space_constraint(x, pltpu.HBM)


def dot_nt(a, b):
    return lax.dot_general(a, b, NT, preferred_element_type=jnp.float32)


def dot_nn(a, b):
    return jnp.dot(a, b, preferred_element_type=jnp.float32)


def span_rows(start):
    row = lax.broadcasted_iota(jnp.int32, (SPAN_ROWS, HEAD_SIZE), 0)
    start = jnp.broadcast_to(start, (SPAN_ROWS, HEAD_SIZE))
    digit = jnp.where(row < SPAN_ROWS // 2, start // HEAD_SIZE, start % HEAD_SIZE)
    return digit.astype(jnp.float32).astype(jnp.bfloat16)


def span_of(rows):
    digits = rows.astype(jnp.float32)
    return digits[0:1, :] * HEAD_SIZE + digits[SPAN_ROWS // 2 : SPAN_ROWS // 2 + 1, :]


def own_bias(doc_row):
    block = doc_row.shape[1]
    row = lax.broadcasted_iota(jnp.int32, (block, block), 0)
    lane = lax.broadcasted_iota(jnp.int32, (block, block), 1)
    along = jnp.broadcast_to(doc_row.astype(jnp.float32), (block, block))
    return jnp.where((lane <= row) & (jnp.transpose(along) == along), 0.0, MASKED_SCORE)


def prepare_kernel(span_ref, *refs):
    sources, (message_ref, *staged), (row, rows_ref, sems) = refs[:3], refs[3:6], refs[6:]
    heads = row.shape[1] // HEAD_SIZE
    copies = [
        pltpu.make_async_copy(source, target, sems.at[i])
        for i, (source, target) in enumerate(zip(sources, (row, *staged)))
    ]
    for copy in copies:
        copy.start()
    copies[0].wait()
    query = row[...].astype(jnp.float32)
    for head in range(heads):
        rows_ref[head : head + 1, :] = query[:, head * HEAD_SIZE : (head + 1) * HEAD_SIZE]
    message_ref[:heads, :] = rows_ref[...].astype(jnp.bfloat16)
    message_ref[heads:, :] = span_rows(span_ref[...].reshape(1, 1))
    for copy in copies[1:]:
        copy.wait()


def prepare(span, query_row, keys, values):
    heads = query_row.shape[1] // HEAD_SIZE
    out_shape = [pltpu.VMEM((heads + SPAN_ROWS, HEAD_SIZE), query_row.dtype)]
    out_shape += [pltpu.VMEM(x.shape, x.dtype) for x in (keys, values)]
    return pl.pallas_call(
        prepare_kernel,
        out_shape=out_shape,
        in_specs=[VMEM] + [HBM] * 3,
        out_specs=[VMEM] * len(out_shape),
        scratch_shapes=[
            pltpu.VMEM(query_row.shape, query_row.dtype),
            pltpu.VMEM((heads, HEAD_SIZE), jnp.float32),
            pltpu.SemaphoreType.DMA((3,)),
        ],
        compiler_params=pltpu.CompilerParams(vmem_limit_bytes=8 * 2**20),
        cost_estimate=pl.CostEstimate(flops=1000, bytes_accessed=600000, transcendentals=0),
        name="prepare",
    )(span, *[in_hbm(x) for x in (query_row, keys, values)])


def stage_kernel(docs_ref, query_ref, bias_ref, staged_ref, docs, sems):
    copies = [
        pltpu.make_async_copy(docs_ref, docs, sems.at[0]),
        pltpu.make_async_copy(query_ref, staged_ref, sems.at[1]),
    ]
    for copy in copies:
        copy.start()
    copies[0].wait()
    bias_ref[...] = own_bias(docs[...])
    copies[1].wait()


def stage(docs, context_queries):
    block = docs.shape[0]
    return pl.pallas_call(
        stage_kernel,
        out_shape=[
            pltpu.VMEM((block, block), jnp.float32),
            pltpu.VMEM(context_queries.shape, context_queries.dtype),
        ],
        in_specs=[HBM] * 2,
        out_specs=[VMEM] * 2,
        scratch_shapes=[pltpu.VMEM((1, block), jnp.int32), pltpu.SemaphoreType.DMA((2,))],
        compiler_params=pltpu.CompilerParams(vmem_limit_bytes=8 * 2**20),
        cost_estimate=pl.CostEstimate(flops=1000, bytes_accessed=2100000, transcendentals=0),
        name="stage",
    )(in_hbm(docs.reshape(1, block)), in_hbm(context_queries))


def partials_kernel(host_ref, k0_ref, v0_ref, k1_ref, v1_ref, *refs):
    message_refs, out_refs = refs[:-2], refs[-2:]
    block = k0_ref.shape[0]
    kv_count = k0_ref.shape[1] // HEAD_SIZE
    heads = message_refs[0].shape[0] - SPAN_ROWS
    per_kv = heads // kv_count
    messages = [message_refs[i][...] for i in (0, 3, 1, 2)]
    rows = len(messages) * heads
    host = host_ref[0]
    queries = jnp.concatenate([message[:heads] for message in messages], 0)
    starts = jnp.concatenate(
        [
            jnp.broadcast_to(span_of(message[heads:]), (heads, HEAD_SIZE))
            for message in messages
        ],
        0,
    )
    row_kv = (lax.broadcasted_iota(jnp.int32, (rows, HEAD_SIZE), 0) % heads) // per_kv
    lanes = lax.broadcasted_iota(jnp.int32, (rows, block), 1)

    def chosen(per_head):
        out = per_head[0]
        for index in range(1, kv_count):
            out = jnp.where(row_kv == index, per_head[index], out)
        return out

    scores, shown = [], []
    for key_ref, at in ((k0_ref, host), (k1_ref, host ^ 1)):
        scores.append(
            chosen(
                [
                    dot_nt(queries, key_ref[:, h * HEAD_SIZE : (h + 1) * HEAD_SIZE])
                    for h in range(kv_count)
                ]
            )
            * FACTOR
        )
        shown.append((lanes + at * block).astype(jnp.float32) >= starts)
    masked = [jnp.where(s, x, MASKED_SCORE) for s, x in zip(shown, scores)]
    peaks = [jnp.max(x, -1, keepdims=True) for x in masked]
    weights = [
        jnp.where(s, jnp.exp(x - p), 0.0) for s, x, p in zip(shown, masked, peaks)
    ]
    peak = jnp.maximum(peaks[0], peaks[1])
    scales = [jnp.exp(p - peak) for p in peaks]
    total, acc = 0.0, 0.0
    for weight, scale, value_ref in zip(weights, scales, (v0_ref, v1_ref)):
        total += scale * jnp.sum(weight, -1, keepdims=True)
        weight = weight.astype(jnp.bfloat16)
        acc += scale * chosen(
            [
                dot_nn(weight, value_ref[:, h * HEAD_SIZE : (h + 1) * HEAD_SIZE])
                for h in range(kv_count)
            ]
        )
    peak_row = jnp.transpose(jnp.broadcast_to(peak, (rows, rows)))[0:1, :]
    total_row = jnp.transpose(jnp.broadcast_to(total, (rows, rows)))[0:1, :]
    acc = acc.astype(jnp.bfloat16)
    row = lax.broadcasted_iota(jnp.int32, (WORD_ROWS, HEAD_SIZE), 0)
    words = jnp.zeros((WORD_ROWS, HEAD_SIZE), jnp.float32)
    for at, rest in ((0, peak_row), (3, total_row)):
        for digit in range(3):
            part = rest.astype(jnp.bfloat16).astype(jnp.float32)
            words = jnp.where(row == at + digit, part, words)
            rest = rest - part
    words = words.astype(jnp.bfloat16)
    size = message_refs[0].shape[0]
    for index in range(len(messages)):
        out_ref, at = out_refs[index // 2], index % 2 * size
        out_ref[at : at + heads, :] = acc[index * heads : (index + 1) * heads]
        out_ref[at + heads : at + size, :] = words


def partials(host, keys, values, other_keys, other_values, messages):
    rows, width = messages[0].shape
    part = pltpu.VMEM((2 * rows, width), messages[0].dtype)
    return pl.pallas_call(
        partials_kernel,
        out_shape=[part] * 2,
        in_specs=[SMEM] + [VMEM] * (4 + len(messages)),
        out_specs=[VMEM] * 2,
        compiler_params=pltpu.CompilerParams(vmem_limit_bytes=8 * 2**20),
        cost_estimate=pl.CostEstimate(flops=1000000, bytes_accessed=900000, transcendentals=40000),
        name="query_partials",
    )(host, keys, values, other_keys, other_values, *messages)


def merged_answer(parts):
    heads = parts[0][0].shape[0] - WORD_ROWS
    row = lax.broadcasted_iota(jnp.int32, (heads, HEAD_SIZE), 0)
    lane = lax.broadcasted_iota(jnp.int32, (heads, HEAD_SIZE), 1)
    peaks, totals, sums = [], [], []
    for part, index in parts:
        sums.append(part[:heads].astype(jnp.float32))
        words = part[heads:].astype(jnp.float32)
        for at, out in ((0, peaks), (3, totals)):
            word = words[at : at + 1, :] + words[at + 1 : at + 2, :] + words[at + 2 : at + 3, :]
            word = jnp.broadcast_to(word, (heads, HEAD_SIZE))
            picked = jnp.where(lane == row + index * heads, word, 0.0)
            out.append(jnp.sum(picked, -1, keepdims=True))
    peak = functools.reduce(jnp.maximum, peaks)
    scales = [jnp.exp(p - peak) for p in peaks]
    total = functools.reduce(jnp.add, [s * t for s, t in zip(scales, totals)])
    merged = functools.reduce(jnp.add, [s * a for s, a in zip(scales, sums)])
    return (merged / total).astype(parts[0][0].dtype)


def chosen_anchor(host_ref, held_ref, arrived_ref, at):
    columns = slice(at, at + HEAD_SIZE)
    odd = jnp.full((held_ref.shape[0], HEAD_SIZE), (host_ref[0] // 2) % 2, jnp.int32)
    return jnp.where(odd == 0, held_ref[:, columns], arrived_ref[:, columns])


def weights_kernel(host_ref, bias_ref, query_ref, key_ref, held_ref, arrived_ref, out_ref):
    block = query_ref.shape[0]
    kv_count = key_ref.shape[1] // HEAD_SIZE
    group = query_ref.shape[1] // key_ref.shape[1]
    scale = FACTOR * LOG2E
    front = jnp.where(host_ref[0] > 0, 0.0, MASKED_SCORE)
    bias = jnp.concatenate([bias_ref[...], jnp.full((block, block), front, jnp.float32)], 1)
    bias = jnp.concatenate([bias] * UNIT, 0)

    def score(first):
        at = first // group * HEAD_SIZE
        far = chosen_anchor(host_ref, held_ref, arrived_ref, at)
        keys = jnp.concatenate([key_ref[:, at : at + HEAD_SIZE], far], 0)
        query = jnp.concatenate(
            [
                query_ref[:, (first + i) * HEAD_SIZE : (first + i + 1) * HEAD_SIZE]
                for i in range(UNIT)
            ],
            0,
        )
        return dot_nt(query, keys)

    def weigh(first, scores):
        scores = scores + bias
        peak = jnp.max(scores, -1, keepdims=True)
        weights = jnp.exp2((scores - peak) * scale)
        out_ref[first * block : (first + UNIT) * block, :] = weights.astype(jnp.bfloat16)

    waiting = None
    for first in range(0, kv_count * group, UNIT):
        scores = score(first)
        if waiting is not None:
            weigh(*waiting)
        waiting = (first, scores)
    weigh(*waiting)


def context_weights(host, bias, queries, keys, held, arrived):
    block, width = queries.shape
    heads = width // HEAD_SIZE
    return pl.pallas_call(
        weights_kernel,
        out_shape=pltpu.VMEM((heads * block, 2 * block), queries.dtype),
        in_specs=[SMEM] + [VMEM] * 5,
        out_specs=VMEM,
        compiler_params=pltpu.CompilerParams(vmem_limit_bytes=16 * 2**20),
        cost_estimate=pl.CostEstimate(
            flops=4 * block * block * width,
            bytes_accessed=4000000,
            transcendentals=2 * heads * block * block,
        ),
        name="context_weights",
    )(host, bias, queries, keys, held, arrived)


def load_kernel(held_ref, kept_ref, back_ref, out_ref):
    block, kv_count = held_ref.shape[0], held_ref.shape[1] // HEAD_SIZE
    size = kept_ref.shape[0] // 2
    for head in range(kv_count):
        columns = slice(head * HEAD_SIZE, (head + 1) * HEAD_SIZE)
        out_ref[head * block : (head + 1) * block, :] = held_ref[:, columns]
    rest = kv_count * block
    out_ref[rest : rest + size, :] = kept_ref[size:, :]
    out_ref[rest + size :, :] = back_ref[size:, :]


def load(held, kept, back):
    rows = held.size // HEAD_SIZE + kept.shape[0]
    return pl.pallas_call(
        load_kernel,
        out_shape=pltpu.VMEM((rows, HEAD_SIZE), held.dtype),
        in_specs=[VMEM] * 3,
        out_specs=VMEM,
        compiler_params=pltpu.CompilerParams(vmem_limit_bytes=8 * 2**20),
        cost_estimate=pl.CostEstimate(flops=1000, bytes_accessed=300000, transcendentals=0),
        name="load",
    )(held, kept, back)


def sums_kernel(answers, host_ref, weight_ref, value_ref, held_ref, arrived_ref, *refs):
    part_refs, scratch = refs[: len(refs) - 4 - answers], refs[-3:]
    out_ref, *answer_refs = refs[len(part_refs) : -3]
    slabs, row, sems = scratch
    kv_count, block, slab = slabs.shape
    group = slab // HEAD_SIZE
    ones = jnp.ones((2 * block, HEAD_SIZE), jnp.bfloat16)
    copies, waiting = [], None
    for answer_ref in answer_refs:
        kept_ref, back_ref = part_refs
        size, rest = kept_ref.shape[0] // 2, kv_count * block
        answer = merged_answer(
            [
                (kept_ref[:size, :], 0),
                (arrived_ref[rest : rest + size, :], 1),
                (back_ref[:size, :], 2),
                (arrived_ref[rest + size :, :], 3),
            ]
        )
        for head in range(answer.shape[0]):
            row[:, head * HEAD_SIZE : (head + 1) * HEAD_SIZE] = answer[head : head + 1, :]
        copies.append(pltpu.make_async_copy(row, answer_ref, sems.at[kv_count]))
        copies[-1].start()

    odd = jnp.full((block, HEAD_SIZE), (host_ref[0] // 2) % 2, jnp.int32)

    def add(first):
        index = first // group
        rows = slice(index * block, (index + 1) * block)
        far = jnp.where(odd == 0, held_ref[rows, :], arrived_ref[rows, :])
        near = value_ref[:, index * HEAD_SIZE : (index + 1) * HEAD_SIZE]
        values = jnp.concatenate([near, far], 0)
        weights = weight_ref[first * block : (first + UNIT) * block, :]
        return dot_nn(weights, jnp.concatenate([values, ones], 1))

    def finish(first, sums):
        total = sums[:, HEAD_SIZE:]
        inverse = pl.reciprocal(total, approx=True)
        inverse = inverse * (2.0 - total * inverse)
        out = (sums[:, :HEAD_SIZE] * inverse).astype(jnp.bfloat16)
        index = first // group
        for i in range(UNIT):
            column = (first % group + i) * HEAD_SIZE
            slabs[index, :, column : column + HEAD_SIZE] = out[i * block : (i + 1) * block, :]
        if first % group + UNIT == group:
            copy = pltpu.make_async_copy(
                slabs.at[index], out_ref.at[:, pl.ds(index * slab, slab)], sems.at[index]
            )
            copy.start()
            copies.append(copy)

    for first in range(0, kv_count * group, UNIT):
        sums = add(first)
        if waiting is not None:
            finish(*waiting)
        waiting = (first, sums)
    finish(*waiting)
    for copy in copies:
        copy.wait()


def context_sums(host, weights, values, held, arrived, parts):
    block, kv_count = values.shape[0], values.shape[1] // HEAD_SIZE
    width = weights.shape[0] // block * HEAD_SIZE
    answers = 1 if parts else 0
    return pl.pallas_call(
        functools.partial(sums_kernel, answers),
        out_shape=[jax.ShapeDtypeStruct((block, width), values.dtype)]
        + [jax.ShapeDtypeStruct((1, width), values.dtype)] * answers,
        in_specs=[SMEM] + [VMEM] * (4 + len(parts)),
        out_specs=[HBM] * (1 + answers),
        scratch_shapes=[
            pltpu.VMEM((kv_count, block, width // kv_count), values.dtype),
            pltpu.VMEM((1, width), values.dtype),
            pltpu.SemaphoreType.DMA((kv_count + 1,)),
        ],
        compiler_params=pltpu.CompilerParams(vmem_limit_bytes=16 * 2**20),
        cost_estimate=pl.CostEstimate(
            flops=4 * block * block * width, bytes_accessed=4000000, transcendentals=0
        ),
        name="context_sums",
    )(host, weights, values, held, arrived, *parts)


def paired(context_queries, context_keys, context_values, doc_ids, query_token_rows, span_start):
    host_count = lax.axis_size("hosts")
    host = lax.axis_index("hosts")
    place, side = host // 2, host % 2

    def swap(value, mask):
        return lax.ppermute(value, "hosts", [(i, i ^ mask) for i in range(host_count)])

    def down(value):
        return lax.ppermute(
            value, "hosts", [(i, i ^ (1 if i // 2 % 2 else 4)) for i in range(host_count)]
        )

    other_keys, other_values = swap(context_keys, 1), swap(context_values, 1)
    message, keys, values = prepare(
        span_start, query_token_rows, context_keys, context_values
    )
    bias, queries = stage(doc_ids, context_queries)

    def descend(own, other):
        first = jnp.where(side == 0, own, other)
        return jnp.where(place == 2, down(first), first)

    messages = [message] + [swap(message, 2 * k) for k in (2, 3, 1)]
    held_keys = descend(keys, other_keys)
    arrived_keys = lax.ppermute(
        held_keys, "hosts", [(i, i ^ 2) for i in range(host_count) if i // 2 % 2 == 0]
    )
    host_word = host.reshape(1).astype(jnp.int32)
    kept, sent = partials(host_word, keys, values, other_keys, other_values, messages)
    back = swap(sent, 4)
    loaded = load(descend(values, other_values), kept, back)
    arrived = swap(loaded, 2)
    weights = context_weights(host_word, bias, queries, keys, held_keys, arrived_keys)
    return tuple(context_sums(host_word, weights, values, loaded, arrived, [kept, back]))


def from_root(value, axis, source):
    kept = jnp.where(lax.axis_index(axis) == source, value, 0).astype(value.dtype)
    return lax.psum(kept, axis)


def head_groups(matrix, kv_count):
    count_rows = matrix.shape[0]
    return matrix.reshape(
        count_rows, kv_count, matrix.shape[1] // (kv_count * HEAD_SIZE), HEAD_SIZE
    ).transpose(1, 0, 2, 3)


def kv_groups(matrix, kv_count):
    return matrix.reshape(matrix.shape[0], kv_count, HEAD_SIZE).transpose(1, 0, 2)


def query_partials(queries, key_rows, value_rows, visible):
    kv_count = key_rows.shape[1] // HEAD_SIZE

    def query_per_head(operands):
        query_part, key_part, value_part = operands
        scores = (
            jnp.einsum("qgd,sd->qgs", query_part, key_part, preferred_element_type=jnp.float32)
            * FACTOR
        )
        shown = visible[:, None, :]
        peak_score = jnp.max(jnp.where(shown, scores, MASKED_SCORE), -1)
        weights = jnp.where(shown, jnp.exp(scores - peak_score[..., None]), 0.0)
        totals = jnp.sum(weights, -1)
        partial_acc = jnp.einsum(
            "qgs,sd->qgd",
            weights.astype(jnp.bfloat16),
            value_part,
            preferred_element_type=jnp.float32,
        )
        return (peak_score, totals, partial_acc)

    peaks, totals, accums = lax.map(
        query_per_head,
        (
            head_groups(queries, kv_count),
            kv_groups(key_rows, kv_count),
            kv_groups(value_rows, kv_count),
        ),
    )
    query_count = queries.shape[0]
    peaks = peaks.transpose(1, 0, 2).reshape(query_count, -1)
    totals = totals.transpose(1, 0, 2).reshape(query_count, -1)
    accums = accums.transpose(1, 0, 2, 3).reshape(query_count, -1)
    return (peaks, totals, accums)


def gathered(context_queries, context_keys, context_values, doc_ids, query_token_rows, span_start):
    host = lax.axis_index("hosts")
    host_count = lax.axis_size("hosts")
    block = context_queries.shape[0]
    per_host = query_token_rows.shape[0]
    anchor = from_root(jnp.stack([context_keys, context_values]), "hosts", 0)
    weights = context_weights(
        host.reshape(1).astype(jnp.int32),
        own_bias(doc_ids.reshape(1, block)),
        context_queries,
        context_keys,
        anchor[0],
        anchor[0],
    )
    kv_count = context_keys.shape[1] // HEAD_SIZE
    by_head = anchor[1].reshape(block, kv_count, HEAD_SIZE).transpose(1, 0, 2)
    by_head = by_head.reshape(kv_count * block, HEAD_SIZE)
    (block_out,) = context_sums(
        host.reshape(1).astype(jnp.int32), weights, context_values, by_head, by_head, []
    )
    all_queries, all_spans = (
        lax.all_gather(query_token_rows, "hosts", axis=0, tiled=True),
        lax.all_gather(span_start, "hosts", axis=0, tiled=True),
    )
    key_positions = host * block + jnp.arange(block, dtype=jnp.int32)
    query_visible = key_positions[None, :] >= all_spans[:, None]
    peaks, totals, accums = query_partials(
        all_queries, context_keys, context_values, query_visible
    )
    received = [
        lax.all_to_all(x, "hosts", split_axis=0, concat_axis=0, tiled=True).reshape(
            host_count, per_host, -1
        )
        for x in (peaks, totals, accums)
    ]
    source_peaks, source_totals, source_accums = received
    overall = jnp.max(source_peaks, 0)
    scales = jnp.exp(source_peaks - overall[None])
    own_totals = jnp.sum(scales * source_totals, 0)
    own_accums = jnp.sum(jnp.repeat(scales, HEAD_SIZE, axis=2) * source_accums, 0)
    answer = (own_accums / jnp.repeat(own_totals, HEAD_SIZE, axis=1)).astype(jnp.bfloat16)
    return (block_out, answer)


def solution(mesh):
    rows = P(("groups", "hosts"), "tensor")
    words = P(("groups", "hosts"))

    def on_device(context_queries, context_keys, context_values, doc_ids, query_rows, span_start):
        kv_count = context_keys.shape[1] // HEAD_SIZE
        fits = mesh.shape["hosts"] == 2 * kv_count and kv_count == 4 and query_rows.shape[0] == 1
        plan = paired if fits else gathered
        return plan(
            context_queries, context_keys, context_values, doc_ids, query_rows, span_start
        )

    return jax.shard_map(
        on_device,
        mesh=mesh,
        in_specs=(rows, rows, rows, words, rows, words),
        out_specs=(rows, rows),
        check_vma=False,
    )
```

```python
import functools

import jax
import jax.numpy as jnp
from jax import lax
from jax.experimental import pallas as pl
from jax.experimental.pallas import tpu as pltpu
from jax.sharding import PartitionSpec as P

HEAD_SIZE = 128
MASKED_SCORE = -1e30
FACTOR = float(HEAD_SIZE) ** -0.5
LOG2E = 1.4426950408889634
VMEM = pl.BlockSpec(memory_space=pltpu.VMEM)
SMEM = pl.BlockSpec(memory_space=pltpu.SMEM)
HBM = pl.BlockSpec(memory_space=pltpu.HBM)
SPAN_ROWS = 16
WORD_ROWS = 16
UNIT = 4
NT = (((1,), (1,)), ((), ()))


def in_hbm(x):
    return pltpu.with_memory_space_constraint(x, pltpu.HBM)


def dot_nt(a, b):
    return lax.dot_general(a, b, NT, preferred_element_type=jnp.float32)


def dot_nn(a, b):
    return jnp.dot(a, b, preferred_element_type=jnp.float32)


def span_rows(start):
    row = lax.broadcasted_iota(jnp.int32, (SPAN_ROWS, HEAD_SIZE), 0)
    start = jnp.broadcast_to(start, (SPAN_ROWS, HEAD_SIZE))
    digit = jnp.where(row < SPAN_ROWS // 2, start // HEAD_SIZE, start % HEAD_SIZE)
    return digit.astype(jnp.float32).astype(jnp.bfloat16)


def span_of(rows):
    digits = rows.astype(jnp.float32)
    return digits[0:1, :] * HEAD_SIZE + digits[SPAN_ROWS // 2 : SPAN_ROWS // 2 + 1, :]


def own_bias(doc_row):
    block = doc_row.shape[1]
    row = lax.broadcasted_iota(jnp.int32, (block, block), 0)
    lane = lax.broadcasted_iota(jnp.int32, (block, block), 1)
    along = jnp.broadcast_to(doc_row.astype(jnp.float32), (block, block))
    return jnp.where((lane <= row) & (jnp.transpose(along) == along), 0.0, MASKED_SCORE)


def prepare_kernel(span_ref, *refs):
    sources, (message_ref, *staged), (row, rows_ref, sems) = refs[:3], refs[3:6], refs[6:]
    heads = row.shape[1] // HEAD_SIZE
    copies = [
        pltpu.make_async_copy(source, target, sems.at[i])
        for i, (source, target) in enumerate(zip(sources, (row, *staged)))
    ]
    for copy in copies:
        copy.start()
    copies[0].wait()
    query = row[...].astype(jnp.float32)
    for head in range(heads):
        rows_ref[head : head + 1, :] = query[:, head * HEAD_SIZE : (head + 1) * HEAD_SIZE]
    message_ref[:heads, :] = rows_ref[...].astype(jnp.bfloat16)
    message_ref[heads:, :] = span_rows(span_ref[...].reshape(1, 1))
    for copy in copies[1:]:
        copy.wait()


def prepare(span, query_row, keys, values):
    heads = query_row.shape[1] // HEAD_SIZE
    out_shape = [pltpu.VMEM((heads + SPAN_ROWS, HEAD_SIZE), query_row.dtype)]
    out_shape += [pltpu.VMEM(x.shape, x.dtype) for x in (keys, values)]
    return pl.pallas_call(
        prepare_kernel,
        out_shape=out_shape,
        in_specs=[VMEM] + [HBM] * 3,
        out_specs=[VMEM] * len(out_shape),
        scratch_shapes=[
            pltpu.VMEM(query_row.shape, query_row.dtype),
            pltpu.VMEM((heads, HEAD_SIZE), jnp.float32),
            pltpu.SemaphoreType.DMA((3,)),
        ],
        compiler_params=pltpu.CompilerParams(vmem_limit_bytes=8 * 2**20),
        cost_estimate=pl.CostEstimate(flops=1000, bytes_accessed=600000, transcendentals=0),
        name="prepare",
    )(span, *[in_hbm(x) for x in (query_row, keys, values)])


def stage_kernel(docs_ref, query_ref, bias_ref, staged_ref, docs, sems):
    copies = [
        pltpu.make_async_copy(docs_ref, docs, sems.at[0]),
        pltpu.make_async_copy(query_ref, staged_ref, sems.at[1]),
    ]
    for copy in copies:
        copy.start()
    copies[0].wait()
    bias_ref[...] = own_bias(docs[...])
    copies[1].wait()


def stage(docs, context_queries):
    block = docs.shape[0]
    return pl.pallas_call(
        stage_kernel,
        out_shape=[
            pltpu.VMEM((block, block), jnp.float32),
            pltpu.VMEM(context_queries.shape, context_queries.dtype),
        ],
        in_specs=[HBM] * 2,
        out_specs=[VMEM] * 2,
        scratch_shapes=[pltpu.VMEM((1, block), jnp.int32), pltpu.SemaphoreType.DMA((2,))],
        compiler_params=pltpu.CompilerParams(vmem_limit_bytes=8 * 2**20),
        cost_estimate=pl.CostEstimate(flops=1000, bytes_accessed=2100000, transcendentals=0),
        name="stage",
    )(in_hbm(docs.reshape(1, block)), in_hbm(context_queries))


def partials_kernel(host_ref, k0_ref, v0_ref, k1_ref, v1_ref, *refs):
    message_refs, out_refs = refs[:-2], refs[-2:]
    block = k0_ref.shape[0]
    kv_count = k0_ref.shape[1] // HEAD_SIZE
    heads = message_refs[0].shape[0] - SPAN_ROWS
    per_kv = heads // kv_count
    messages = [message_refs[i][...] for i in (0, 2, 3, 1)]
    rows = len(messages) * heads
    host = host_ref[0]
    queries = jnp.concatenate([message[:heads] for message in messages], 0)
    starts = jnp.concatenate(
        [
            jnp.broadcast_to(span_of(message[heads:]), (heads, HEAD_SIZE))
            for message in messages
        ],
        0,
    )
    row_kv = (lax.broadcasted_iota(jnp.int32, (rows, HEAD_SIZE), 0) % heads) // per_kv
    lanes = lax.broadcasted_iota(jnp.int32, (rows, block), 1)

    def chosen(per_head):
        out = per_head[0]
        for index in range(1, kv_count):
            out = jnp.where(row_kv == index, per_head[index], out)
        return out

    scores, shown = [], []
    for key_ref, at in ((k0_ref, host), (k1_ref, host ^ 1)):
        scores.append(
            chosen(
                [
                    dot_nt(queries, key_ref[:, h * HEAD_SIZE : (h + 1) * HEAD_SIZE])
                    for h in range(kv_count)
                ]
            )
            * FACTOR
        )
        shown.append((lanes + at * block).astype(jnp.float32) >= starts)
    masked = [jnp.where(s, x, MASKED_SCORE) for s, x in zip(shown, scores)]
    peaks = [jnp.max(x, -1, keepdims=True) for x in masked]
    weights = [
        jnp.where(s, jnp.exp(x - p), 0.0) for s, x, p in zip(shown, masked, peaks)
    ]
    peak = jnp.maximum(peaks[0], peaks[1])
    scales = [jnp.exp(p - peak) for p in peaks]
    total, acc = 0.0, 0.0
    for weight, scale, value_ref in zip(weights, scales, (v0_ref, v1_ref)):
        total += scale * jnp.sum(weight, -1, keepdims=True)
        weight = weight.astype(jnp.bfloat16)
        acc += scale * chosen(
            [
                dot_nn(weight, value_ref[:, h * HEAD_SIZE : (h + 1) * HEAD_SIZE])
                for h in range(kv_count)
            ]
        )
    peak_row = jnp.transpose(jnp.broadcast_to(peak, (rows, rows)))[0:1, :]
    total_row = jnp.transpose(jnp.broadcast_to(total, (rows, rows)))[0:1, :]
    acc = acc.astype(jnp.bfloat16)
    row = lax.broadcasted_iota(jnp.int32, (WORD_ROWS, HEAD_SIZE), 0)
    words = jnp.zeros((WORD_ROWS, HEAD_SIZE), jnp.float32)
    for at, rest in ((0, peak_row), (3, total_row)):
        for digit in range(3):
            part = rest.astype(jnp.bfloat16).astype(jnp.float32)
            words = jnp.where(row == at + digit, part, words)
            rest = rest - part
    words = words.astype(jnp.bfloat16)
    size = message_refs[0].shape[0]
    for index in range(len(messages)):
        out_ref, at = out_refs[index // 2], index % 2 * size
        out_ref[at : at + heads, :] = acc[index * heads : (index + 1) * heads]
        out_ref[at + heads : at + size, :] = words


def partials(host, keys, values, other_keys, other_values, messages):
    rows, width = messages[0].shape
    part = pltpu.VMEM((2 * rows, width), messages[0].dtype)
    return pl.pallas_call(
        partials_kernel,
        out_shape=[part] * 2,
        in_specs=[SMEM] + [VMEM] * (4 + len(messages)),
        out_specs=[VMEM] * 2,
        compiler_params=pltpu.CompilerParams(vmem_limit_bytes=8 * 2**20),
        cost_estimate=pl.CostEstimate(flops=1000000, bytes_accessed=900000, transcendentals=40000),
        name="query_partials",
    )(host, keys, values, other_keys, other_values, *messages)


def merged_answer(parts):
    heads = parts[0][0].shape[0] - WORD_ROWS
    row = lax.broadcasted_iota(jnp.int32, (heads, HEAD_SIZE), 0)
    lane = lax.broadcasted_iota(jnp.int32, (heads, HEAD_SIZE), 1)
    peaks, totals, sums = [], [], []
    for part, index in parts:
        sums.append(part[:heads].astype(jnp.float32))
        words = part[heads:].astype(jnp.float32)
        for at, out in ((0, peaks), (3, totals)):
            word = words[at : at + 1, :] + words[at + 1 : at + 2, :] + words[at + 2 : at + 3, :]
            word = jnp.broadcast_to(word, (heads, HEAD_SIZE))
            picked = jnp.where(lane == row + index * heads, word, 0.0)
            out.append(jnp.sum(picked, -1, keepdims=True))
    peak = functools.reduce(jnp.maximum, peaks)
    scales = [jnp.exp(p - peak) for p in peaks]
    total = functools.reduce(jnp.add, [s * t for s, t in zip(scales, totals)])
    merged = functools.reduce(jnp.add, [s * a for s, a in zip(scales, sums)])
    return (merged / total).astype(parts[0][0].dtype)


def chosen_anchor(host_ref, held_ref, arrived_ref, at):
    columns = slice(at, at + HEAD_SIZE)
    odd = jnp.full((held_ref.shape[0], HEAD_SIZE), (host_ref[0] // 2) % 2, jnp.int32)
    return jnp.where(odd == 0, held_ref[:, columns], arrived_ref[:, columns])


def weights_kernel(host_ref, bias_ref, query_ref, key_ref, held_ref, arrived_ref, out_ref):
    block = query_ref.shape[0]
    kv_count = key_ref.shape[1] // HEAD_SIZE
    group = query_ref.shape[1] // key_ref.shape[1]
    scale = FACTOR * LOG2E
    front = jnp.where(host_ref[0] > 0, 0.0, MASKED_SCORE)
    bias = jnp.concatenate([bias_ref[...], jnp.full((block, block), front, jnp.float32)], 1)
    bias = jnp.concatenate([bias] * UNIT, 0)

    def score(first):
        at = first // group * HEAD_SIZE
        far = chosen_anchor(host_ref, held_ref, arrived_ref, at)
        keys = jnp.concatenate([key_ref[:, at : at + HEAD_SIZE], far], 0)
        query = jnp.concatenate(
            [
                query_ref[:, (first + i) * HEAD_SIZE : (first + i + 1) * HEAD_SIZE]
                for i in range(UNIT)
            ],
            0,
        )
        return dot_nt(query, keys)

    def weigh(first, scores):
        scores = scores + bias
        peak = jnp.max(scores, -1, keepdims=True)
        weights = jnp.exp2((scores - peak) * scale)
        out_ref[first * block : (first + UNIT) * block, :] = weights.astype(jnp.bfloat16)

    waiting = None
    for first in range(0, kv_count * group, UNIT):
        scores = score(first)
        if waiting is not None:
            weigh(*waiting)
        waiting = (first, scores)
    weigh(*waiting)


def context_weights(host, bias, queries, keys, held, arrived):
    block, width = queries.shape
    heads = width // HEAD_SIZE
    return pl.pallas_call(
        weights_kernel,
        out_shape=pltpu.VMEM((heads * block, 2 * block), queries.dtype),
        in_specs=[SMEM] + [VMEM] * 5,
        out_specs=VMEM,
        compiler_params=pltpu.CompilerParams(vmem_limit_bytes=16 * 2**20),
        cost_estimate=pl.CostEstimate(
            flops=4 * block * block * width,
            bytes_accessed=4000000,
            transcendentals=2 * heads * block * block,
        ),
        name="context_weights",
    )(host, bias, queries, keys, held, arrived)


def load_kernel(held_ref, kept_ref, back_ref, out_ref):
    block, kv_count = held_ref.shape[0], held_ref.shape[1] // HEAD_SIZE
    size = kept_ref.shape[0] // 2
    for head in range(kv_count):
        columns = slice(head * HEAD_SIZE, (head + 1) * HEAD_SIZE)
        out_ref[head * block : (head + 1) * block, :] = held_ref[:, columns]
    rest = kv_count * block
    out_ref[rest : rest + size, :] = kept_ref[size:, :]
    out_ref[rest + size :, :] = back_ref[size:, :]


def load(held, kept, back):
    rows = held.size // HEAD_SIZE + kept.shape[0]
    return pl.pallas_call(
        load_kernel,
        out_shape=pltpu.VMEM((rows, HEAD_SIZE), held.dtype),
        in_specs=[VMEM] * 3,
        out_specs=VMEM,
        compiler_params=pltpu.CompilerParams(vmem_limit_bytes=8 * 2**20),
        cost_estimate=pl.CostEstimate(flops=1000, bytes_accessed=300000, transcendentals=0),
        name="load",
    )(held, kept, back)


def sums_kernel(answers, host_ref, weight_ref, value_ref, held_ref, arrived_ref, *refs):
    part_refs, scratch = refs[: len(refs) - 4 - answers], refs[-3:]
    out_ref, *answer_refs = refs[len(part_refs) : -3]
    slabs, row, sems = scratch
    kv_count, block, slab = slabs.shape
    group = slab // HEAD_SIZE
    ones = jnp.ones((2 * block, HEAD_SIZE), jnp.bfloat16)
    copies, waiting = [], None
    for answer_ref in answer_refs:
        kept_ref, back_ref = part_refs
        size, rest = kept_ref.shape[0] // 2, kv_count * block
        answer = merged_answer(
            [
                (kept_ref[:size, :], 0),
                (arrived_ref[rest : rest + size, :], 1),
                (back_ref[:size, :], 2),
                (arrived_ref[rest + size :, :], 3),
            ]
        )
        for head in range(answer.shape[0]):
            row[:, head * HEAD_SIZE : (head + 1) * HEAD_SIZE] = answer[head : head + 1, :]
        copies.append(pltpu.make_async_copy(row, answer_ref, sems.at[kv_count]))
        copies[-1].start()

    odd = jnp.full((block, HEAD_SIZE), (host_ref[0] // 2) % 2, jnp.int32)

    def add(first):
        index = first // group
        rows = slice(index * block, (index + 1) * block)
        far = jnp.where(odd == 0, held_ref[rows, :], arrived_ref[rows, :])
        near = value_ref[:, index * HEAD_SIZE : (index + 1) * HEAD_SIZE]
        values = jnp.concatenate([near, far], 0)
        weights = weight_ref[first * block : (first + UNIT) * block, :]
        return dot_nn(weights, jnp.concatenate([values, ones], 1))

    def finish(first, sums):
        total = sums[:, HEAD_SIZE:]
        inverse = pl.reciprocal(total, approx=True)
        inverse = inverse * (2.0 - total * inverse)
        out = (sums[:, :HEAD_SIZE] * inverse).astype(jnp.bfloat16)
        index = first // group
        for i in range(UNIT):
            column = (first % group + i) * HEAD_SIZE
            slabs[index, :, column : column + HEAD_SIZE] = out[i * block : (i + 1) * block, :]
        if first % group + UNIT == group:
            copy = pltpu.make_async_copy(
                slabs.at[index], out_ref.at[:, pl.ds(index * slab, slab)], sems.at[index]
            )
            copy.start()
            copies.append(copy)

    for first in range(0, kv_count * group, UNIT):
        sums = add(first)
        if waiting is not None:
            finish(*waiting)
        waiting = (first, sums)
    finish(*waiting)
    for copy in copies:
        copy.wait()


def context_sums(host, weights, values, held, arrived, parts):
    block, kv_count = values.shape[0], values.shape[1] // HEAD_SIZE
    width = weights.shape[0] // block * HEAD_SIZE
    answers = 1 if parts else 0
    return pl.pallas_call(
        functools.partial(sums_kernel, answers),
        out_shape=[jax.ShapeDtypeStruct((block, width), values.dtype)]
        + [jax.ShapeDtypeStruct((1, width), values.dtype)] * answers,
        in_specs=[SMEM] + [VMEM] * (4 + len(parts)),
        out_specs=[HBM] * (1 + answers),
        scratch_shapes=[
            pltpu.VMEM((kv_count, block, width // kv_count), values.dtype),
            pltpu.VMEM((1, width), values.dtype),
            pltpu.SemaphoreType.DMA((kv_count + 1,)),
        ],
        compiler_params=pltpu.CompilerParams(vmem_limit_bytes=16 * 2**20),
        cost_estimate=pl.CostEstimate(
            flops=4 * block * block * width, bytes_accessed=4000000, transcendentals=0
        ),
        name="context_sums",
    )(host, weights, values, held, arrived, *parts)


def paired(context_queries, context_keys, context_values, doc_ids, query_token_rows, span_start):
    host_count = lax.axis_size("hosts")
    host = lax.axis_index("hosts")
    place, side = host // 2, host % 2

    def swap(value, mask):
        return lax.ppermute(value, "hosts", [(i, i ^ mask) for i in range(host_count)])

    def down(value):
        return lax.ppermute(
            value, "hosts", [(i, i ^ (1 if i // 2 % 2 else 4)) for i in range(host_count)]
        )

    other_keys, other_values = swap(context_keys, 1), swap(context_values, 1)
    message, keys, values = prepare(
        span_start, query_token_rows, context_keys, context_values
    )
    bias, queries = stage(doc_ids, context_queries)

    def descend(own, other):
        first = jnp.where(side == 0, own, other)
        return jnp.where(place == 2, down(first), first)

    messages = [message] + [swap(message, 2 * k) for k in (3, 1, 2)]
    held_keys = descend(keys, other_keys)
    arrived_keys = lax.ppermute(
        held_keys, "hosts", [(i, i ^ 2) for i in range(host_count) if i // 2 % 2 == 0]
    )
    host_word = host.reshape(1).astype(jnp.int32)
    kept, sent = partials(host_word, keys, values, other_keys, other_values, messages)
    back = swap(sent, 4)
    loaded = load(descend(values, other_values), kept, back)
    arrived = swap(loaded, 2)
    weights = context_weights(host_word, bias, queries, keys, held_keys, arrived_keys)
    return tuple(context_sums(host_word, weights, values, loaded, arrived, [kept, back]))


def from_root(value, axis, source):
    kept = jnp.where(lax.axis_index(axis) == source, value, 0).astype(value.dtype)
    return lax.psum(kept, axis)


def head_groups(matrix, kv_count):
    count_rows = matrix.shape[0]
    return matrix.reshape(
        count_rows, kv_count, matrix.shape[1] // (kv_count * HEAD_SIZE), HEAD_SIZE
    ).transpose(1, 0, 2, 3)


def kv_groups(matrix, kv_count):
    return matrix.reshape(matrix.shape[0], kv_count, HEAD_SIZE).transpose(1, 0, 2)


def query_partials(queries, key_rows, value_rows, visible):
    kv_count = key_rows.shape[1] // HEAD_SIZE

    def query_per_head(operands):
        query_part, key_part, value_part = operands
        scores = (
            jnp.einsum("qgd,sd->qgs", query_part, key_part, preferred_element_type=jnp.float32)
            * FACTOR
        )
        shown = visible[:, None, :]
        peak_score = jnp.max(jnp.where(shown, scores, MASKED_SCORE), -1)
        weights = jnp.where(shown, jnp.exp(scores - peak_score[..., None]), 0.0)
        totals = jnp.sum(weights, -1)
        partial_acc = jnp.einsum(
            "qgs,sd->qgd",
            weights.astype(jnp.bfloat16),
            value_part,
            preferred_element_type=jnp.float32,
        )
        return (peak_score, totals, partial_acc)

    peaks, totals, accums = lax.map(
        query_per_head,
        (
            head_groups(queries, kv_count),
            kv_groups(key_rows, kv_count),
            kv_groups(value_rows, kv_count),
        ),
    )
    query_count = queries.shape[0]
    peaks = peaks.transpose(1, 0, 2).reshape(query_count, -1)
    totals = totals.transpose(1, 0, 2).reshape(query_count, -1)
    accums = accums.transpose(1, 0, 2, 3).reshape(query_count, -1)
    return (peaks, totals, accums)


def gathered(context_queries, context_keys, context_values, doc_ids, query_token_rows, span_start):
    host = lax.axis_index("hosts")
    host_count = lax.axis_size("hosts")
    block = context_queries.shape[0]
    per_host = query_token_rows.shape[0]
    anchor = from_root(jnp.stack([context_keys, context_values]), "hosts", 0)
    weights = context_weights(
        host.reshape(1).astype(jnp.int32),
        own_bias(doc_ids.reshape(1, block)),
        context_queries,
        context_keys,
        anchor[0],
        anchor[0],
    )
    kv_count = context_keys.shape[1] // HEAD_SIZE
    by_head = anchor[1].reshape(block, kv_count, HEAD_SIZE).transpose(1, 0, 2)
    by_head = by_head.reshape(kv_count * block, HEAD_SIZE)
    (block_out,) = context_sums(
        host.reshape(1).astype(jnp.int32), weights, context_values, by_head, by_head, []
    )
    all_queries, all_spans = (
        lax.all_gather(query_token_rows, "hosts", axis=0, tiled=True),
        lax.all_gather(span_start, "hosts", axis=0, tiled=True),
    )
    key_positions = host * block + jnp.arange(block, dtype=jnp.int32)
    query_visible = key_positions[None, :] >= all_spans[:, None]
    peaks, totals, accums = query_partials(
        all_queries, context_keys, context_values, query_visible
    )
    received = [
        lax.all_to_all(x, "hosts", split_axis=0, concat_axis=0, tiled=True).reshape(
            host_count, per_host, -1
        )
        for x in (peaks, totals, accums)
    ]
    source_peaks, source_totals, source_accums = received
    overall = jnp.max(source_peaks, 0)
    scales = jnp.exp(source_peaks - overall[None])
    own_totals = jnp.sum(scales * source_totals, 0)
    own_accums = jnp.sum(jnp.repeat(scales, HEAD_SIZE, axis=2) * source_accums, 0)
    answer = (own_accums / jnp.repeat(own_totals, HEAD_SIZE, axis=1)).astype(jnp.bfloat16)
    return (block_out, answer)


def solution(mesh):
    rows = P(("groups", "hosts"), "tensor")
    words = P(("groups", "hosts"))

    def on_device(context_queries, context_keys, context_values, doc_ids, query_rows, span_start):
        kv_count = context_keys.shape[1] // HEAD_SIZE
        fits = mesh.shape["hosts"] == 2 * kv_count and kv_count == 4 and query_rows.shape[0] == 1
        plan = paired if fits else gathered
        return plan(
            context_queries, context_keys, context_values, doc_ids, query_rows, span_start
        )

    return jax.shard_map(
        on_device,
        mesh=mesh,
        in_specs=(rows, rows, rows, words, rows, words),
        out_specs=(rows, rows),
        check_vma=False,
    )
```
